32 devices in a mesh: ctx: 8 (over y, x, core), grp: 4 (over z).
Axes of the slice: x: 2, y: 2, z: 4, core: 2. Of those that a mesh axis runs over, the one named last changes fastest.
Arguments:
- tokens: bfloat16 [8192, 2560], P(('ctx', 'grp')), may hold values from -6 to 6
- norm_gain: bfloat16 [2560], replicated, may hold values from 0.5 to 1.5
- w_query: bfloat16 [2560, 2560], P('grp'), may hold values from -0.125 to 0.125
- w_key: bfloat16 [2560, 512], P('grp'), may hold values from -0.125 to 0.125
- w_value: bfloat16 [2560, 512], P('grp'), may hold values from -0.125 to 0.125
- b_query: bfloat16 [2560], replicated, may hold values from -3 to 3
- b_key: bfloat16 [512], replicated, may hold values from -3 to 3
- b_value: bfloat16 [512], replicated, may hold values from -3 to 3
- cache_keys: bfloat16 [1024, 512], P('ctx'), may hold values from -140 to 140
- cache_values: bfloat16 [1024, 512], P('ctx'), may hold values from -6 to 6
- block_lists: int32 [20, 64, 4], P(None, ('ctx', 'grp')), may hold values from -1 to 7, as said below
- start_position: int32 [1], replicated, may hold values from 0 to 1040384
Outputs:
- context: float32 [8192, 2560], P(('ctx', 'grp'))
- keys_new: float32 [8192, 512], P(('ctx', 'grp'))
- values_new: float32 [8192, 512], P(('ctx', 'grp'))
The draws below stay inside these ranges and needn't reach their ends.
Inputs may be any that keep to these rules, and one draw needn't show every extreme that they name: `block_lists`: each list names distinct blocks of 128 prefix positions, named blocks first and -1 in the empty slots after them; every list names at least one block, some list names 4 and some only one.
All inputs are finite; a program needn't handle non-finite values.
Results may differ from the reference program's by a relative error of at most 0.034.
Values may be sent and summed in bfloat16 or wider, within the bound.
No kernel may reach another device: no remote copies, remote signals or barrier semaphores. Data moves between devices by JAX's collectives and lax.ppermute only.
A program may use at most 128 MiB of HBM per device.

```python
import jax
import jax.numpy as jnp
import numpy as np
from jax import lax

D = 2560
HD = 128
KVH = 4
GROUP = 5
QBLK = 128
SEL = 4
ASKER_CHANNELS = 20
TOKENS = 8192
PREFIX = 1024
NQB = 64
LEADING_TILES = 8


def draw_block_lists(key, part):
    key_noise, key_vertical, lookup_self_share, key_count = jax.random.split(key, 4)
    noisy_affinity_share = jax.random.randint(key_noise, (ASKER_CHANNELS, NQB, LEADING_TILES), 0, 1000)
    vertical_band = (jax.random.randint(key_vertical, (ASKER_CHANNELS, 1, LEADING_TILES), 0, 5) == 0).astype(jnp.int32) * 1500
    latest_element = (jnp.arange(LEADING_TILES) == LEADING_TILES - 1).astype(jnp.int32)
    self_match_reward = jax.random.randint(lookup_self_share, (ASKER_CHANNELS, 1, 1), 0, 2) * 3000
    self_match_reward = self_match_reward.at[0].set(3000)
    attention_affinity = (noisy_affinity_share + vertical_band + self_match_reward * latest_element[None, None, :]) * LEADING_TILES + jnp.arange(LEADING_TILES, dtype=jnp.int32)[None, None, :]
    chosen = lax.top_k(attention_affinity, SEL)[1].astype(jnp.int32)
    counts = jax.random.randint(key_count, (ASKER_CHANNELS, NQB, 1), 1, SEL + 1)
    counts = counts.at[0, 0, 0].set(SEL).at[0, NQB - 1, 0].set(1)
    slot_index = jnp.arange(SEL, dtype=jnp.int32)[None, None, :]
    return jnp.where(slot_index < counts, chosen, -1).astype(jnp.int32)


def draw_cache_keys(key, part):
    key_base = jax.random.fold_in(key, 0)
    width_all = KVH * HD
    return jax.random.truncated_normal(key_base, -4.0, 4.0, (PREFIX, width_all), jnp.float32).astype(jnp.bfloat16)


def block_scale(stream_key, shape, cuts, low, largest):
    factor_of = 1.0
    for axis_at, blocks in cuts:
        heights = jax.random.uniform(jax.random.fold_in(jax.random.fold_in(stream_key, 6), axis_at), (blocks,), jnp.float32, low / len(cuts), largest / len(cuts))
        factor_of = factor_of * jnp.repeat(jnp.exp(heights), shape[axis_at] // blocks).reshape((-1,) + (1,) * (len(shape) - 1 - axis_at))
    return factor_of


def centred(stream_key, dims, scale, bound, cuts=(), held_as=jnp.bfloat16):
    values = jax.random.normal(stream_key, dims, jnp.float32) * scale
    if len(cuts) > 0:
        values = block_scale(stream_key, dims, cuts, -0.22, 0.18) * values
    return jnp.clip(values, min=-bound, max=bound).astype(held_as)


def setup_inputs(seed: int = 0) -> dict:
    streams_of = jax.random.split(jax.random.key(seed), 13)
    return {
        "tokens": centred(streams_of[0], (TOKENS, D), 1.0, 6.0, ((0, 32),)),
        "norm_gain": jnp.clip(1.0 + 0.1 * jax.random.normal(streams_of[1], (D,), jnp.float32), 0.5, 1.5).astype(jnp.bfloat16),
        "w_query": centred(streams_of[2], (D, ASKER_CHANNELS * HD), D ** -0.5, 0.125, ((0, 4),)),
        "w_key": centred(streams_of[3], (D, KVH * HD), D ** -0.5, 0.125, ((0, 4),)),
        "w_value": centred(streams_of[4], (D, KVH * HD), D ** -0.5, 0.125, ((0, 4),)),
        "b_query": centred(streams_of[5], (ASKER_CHANNELS * HD,), 0.5, 3.0),
        "b_key": centred(streams_of[6], (KVH * HD,), 0.5, 3.0),
        "b_value": centred(streams_of[7], (KVH * HD,), 0.5, 3.0),
        "cache_keys": draw_cache_keys(jax.random.fold_in(streams_of[12], 71), 0),
        "cache_values": centred(streams_of[9], (PREFIX, KVH * HD), 1.0, 6.0, ((0, 8),)),
        "block_lists": draw_block_lists(jax.random.fold_in(streams_of[12], 71), 0),
        "start_position": jax.random.randint(streams_of[11], (1,), 0, 1048576 - TOKENS + 1).astype(jnp.int32),
    }


norm_eps = 1e-06
rope_base = 10000000.0

def angle_tables(head_dim):
    half_dim = head_dim // 2
    frequency = rope_base ** (-2.0 * np.arange(half_dim) / head_dim)
    return np.stack([np.mod(frequency * 32.0 ** digit_level, 2.0 * np.pi) for digit_level in range(4)])

def rotate(values, positions):
    head_dim = values.shape[-1]
    half_dim = head_dim // 2
    tables = jnp.asarray(angle_tables(head_dim), jnp.float32)
    angles = jnp.zeros((positions.shape[0], half_dim), jnp.float32)
    remaining = positions
    for digit_level in range(4):
        digit_value = (remaining % 32).astype(jnp.float32)
        angles = angles + digit_value[:, None] * tables[digit_level][None, :]
        remaining = remaining // 32
    cosine = jnp.cos(angles)[:, None, :]
    sine_part = jnp.sin(angles)[:, None, :]
    lower_half = values[..., :half_dim]
    upper_half = values[..., half_dim:]
    return jnp.concatenate([lower_half * cosine - upper_half * sine_part, upper_half * cosine + lower_half * sine_part], axis=-1)

def reference(tokens, norm_gain, w_query, w_key, w_value, b_query, b_key, b_value, cache_keys, cache_values, block_lists, start_position):
    widened = tokens.astype(jnp.float32)
    normed = (widened * lax.rsqrt(lax.optimization_barrier(jnp.mean(widened * widened, axis=-1, keepdims=True)) + norm_eps) * norm_gain.astype(jnp.float32)).astype(jnp.bfloat16)
    query_lin = jnp.dot(normed, w_query, preferred_element_type=jnp.float32) + b_query.astype(jnp.float32)
    key_lin = jnp.dot(normed, w_key, preferred_element_type=jnp.float32) + b_key.astype(jnp.float32)
    value_lin = jnp.dot(normed, w_value, preferred_element_type=jnp.float32) + b_value.astype(jnp.float32)
    positions = start_position[0] + jnp.arange(TOKENS, dtype=jnp.int32)
    query = rotate(query_lin.reshape(TOKENS, ASKER_CHANNELS, HD), positions)
    keys_new = rotate(key_lin.reshape(TOKENS, KVH, HD), positions).reshape(TOKENS, KVH * HD)
    values_new = value_lin
    score_scale = HD ** (-0.5)
    prefix_keys = cache_keys.astype(jnp.float32).reshape(PREFIX, KVH, HD)
    prefix_values = cache_values.astype(jnp.float32).reshape(PREFIX, KVH, HD)
    block_index = jnp.arange(LEADING_TILES, dtype=jnp.int32)
    causal = jnp.arange(QBLK)[:, None] >= jnp.arange(QBLK)[None, :]

    def one_block(inputs):
        query_block, key_block, value_block, list_block = inputs
        far_scores = jnp.einsum('qkgd,pkd->kgqp', query_block, prefix_keys) * score_scale
        listed = jnp.any(list_block[:, :, None] == block_index[None, None, :], axis=1).reshape(KVH, GROUP, 1, LEADING_TILES, 1)
        far_scores = jnp.where(listed, far_scores.reshape(KVH, GROUP, QBLK, LEADING_TILES, QBLK), -jnp.inf).reshape(KVH, GROUP, QBLK, PREFIX)
        near_scores = jnp.einsum('qkgd,skd->kgqs', query_block, key_block) * score_scale
        near_scores = jnp.where(causal, near_scores, -jnp.inf)
        row_max = jnp.maximum(lax.optimization_barrier(jnp.max(far_scores, axis=-1)), lax.optimization_barrier(jnp.max(near_scores, axis=-1)))
        far_exp = jnp.exp(far_scores - row_max[..., None])
        near_exp = jnp.exp(near_scores - row_max[..., None])
        row_sum = lax.optimization_barrier(jnp.sum(far_exp, axis=-1)) + lax.optimization_barrier(jnp.sum(near_exp, axis=-1))
        mixed = jnp.einsum('kgqp,pkd->qkgd', far_exp, prefix_values)
        mixed = mixed + jnp.einsum('kgqs,skd->qkgd', near_exp, value_block)
        return (mixed / jnp.transpose(row_sum, (2, 0, 1))[..., None]).reshape(QBLK, ASKER_CHANNELS * HD)
    query_blocks = query.reshape(NQB, QBLK, KVH, GROUP, HD)
    key_blocks = keys_new.reshape(NQB, QBLK, KVH, HD)
    value_blocks = values_new.reshape(NQB, QBLK, KVH, HD)
    list_blocks = jnp.transpose(block_lists, (1, 0, 2))
    context = lax.map(one_block, (query_blocks, key_blocks, value_blocks, list_blocks)).reshape(TOKENS, ASKER_CHANNELS * HD)
    return (context, keys_new, values_new)
```

```python
import functools

import jax
import jax.numpy as jnp
import numpy as np
from jax import lax
from jax.experimental import pallas as pl
from jax.experimental.pallas import tpu as pltpu
from jax.sharding import PartitionSpec as P

HD = 128
GROUP = 5
QBLK = 128
SEL = 4
TEAM = 4

norm_eps = 1e-06
rope_base = 10000000.0

CHUNKS = ((0, 2), (2, 4), (4, 6), (6, 7))


def angle_tables(head_dim):
    half_dim = head_dim // 2
    frequency = rope_base ** (-2.0 * np.arange(half_dim) / head_dim)
    return np.stack(
        [np.mod(frequency * 32.0**digit_level, 2.0 * np.pi) for digit_level in range(4)]
    )


def rope_tables(positions):
    tables = jnp.asarray(np.tile(angle_tables(HD), (1, 2)), jnp.float32)
    angles = jnp.zeros((positions.shape[0], HD), jnp.float32)
    remaining = positions
    for digit_level in range(4):
        digit_value = (remaining % 32).astype(jnp.float32)
        angles = angles + digit_value[:, None] * tables[digit_level][None, :]
        remaining = remaining // 32
    sign = jnp.where(jnp.arange(HD) < HD // 2, -1.0, 1.0).astype(jnp.float32)
    return jnp.cos(angles), jnp.sin(angles) * sign


def swap(value, axis, bit):
    size = lax.axis_size(axis)
    return lax.ppermute(value, axis, [(i, i ^ bit) for i in range(size)])


def bits_of(size, low):
    bits = []
    bit = low
    while bit < size:
        bits.append(bit)
        bit *= 2
    return bits[::-1]


def turned(value, cosine, sine):
    return value * cosine + pltpu.roll(value, HD // 2, 1) * sine


def heads_kernel(tiles, piece_count, piece_rows, *refs):
    first_tile, last_tile = tiles
    has_kv = first_tile == 0
    query_first = max(first_tile, 2)
    query_count = last_tile - query_first
    width = (last_tile - first_tile) * HD
    refs = list(refs)

    def take(count):
        taken = refs[:count]
        del refs[:count]
        return taken

    (offsets_ref,) = take(1)
    if query_count:
        (lists_ref,) = take(1)
    x_refs = take(TEAM)
    piece_refs = take(piece_count)
    wq_ref, wk_ref, wv_ref = take(3)
    bias_ref, cosine_ref, sine_ref = take(3)
    if query_count:
        (cache_ref,) = take(1)
    if not has_kv:
        (kv_ref,) = take(1)
    if has_kv:
        kv_own_ref, kv_ref = take(2)
    if query_count:
        out_refs = take(TEAM)
    x_buf, w_buf, x_sem, w_sem = take(4)
    if query_count:
        q_buf, o_buf = take(2)

    rows = x_refs[0].shape[0]
    shard = wq_ref.shape[0]
    group = offsets_ref[0]
    local = pl.ds(pl.multiple_of(offsets_ref[1], 16), shard)
    copies = []
    if has_kv:
        column = pl.ds(pl.multiple_of(group * HD, HD), HD)
        copies.append((wk_ref.at[:, column], w_buf.at[local, pl.ds(0, HD)]))
        copies.append((wv_ref.at[:, column], w_buf.at[local, pl.ds(HD, HD)]))
    if query_count:
        column = pl.ds(
            pl.multiple_of((group * GROUP + query_first - 2) * HD, HD), query_count * HD
        )
        copies.append(
            (
                wq_ref.at[:, column],
                w_buf.at[local, pl.ds((query_first - first_tile) * HD, query_count * HD)],
            )
        )
    for index, piece in enumerate(piece_refs):
        start = pl.multiple_of(offsets_ref[2 + index], 16)
        copies.append((piece, w_buf.at[pl.ds(start, piece_rows), :]))
    copies = [
        pltpu.make_async_copy(source, target, w_sem.at[index])
        for index, (source, target) in enumerate(copies)
    ]
    x_copies = [
        pltpu.make_async_copy(x_refs[r], x_buf.at[pl.ds(r * rows, rows), :], x_sem.at[r])
        for r in range(TEAM)
    ]
    for copy in copies:
        copy.start()
    for copy in x_copies:
        copy.start()
    for copy in copies:
        copy.wait()
    for r in range(TEAM):
        x_copies[r].wait()
        span = pl.ds(r * rows, rows)
        lin = (
            jnp.dot(x_buf[span, :], w_buf[...], preferred_element_type=jnp.float32)
            + bias_ref[...]
        )
        cosine, sine = cosine_ref[span, :], sine_ref[span, :]
        for tile in range(first_tile, last_tile):
            at = (tile - first_tile) * HD
            value = lin[:, at : at + HD]
            if tile != 1:
                value = turned(value, cosine, sine)
            if tile >= 2:
                q_buf[span, pl.ds((tile - query_first) * HD, HD)] = value.astype(jnp.bfloat16)
            else:
                kv_ref[span, pl.ds(at, HD)] = value.astype(jnp.bfloat16)
                if r == 0:
                    kv_own_ref[:, pl.ds(at, HD)] = value
    if not query_count:
        return

    scale = HD ** (-0.5)
    causal = lax.broadcasted_iota(jnp.int32, (QBLK, QBLK), 0) >= lax.broadcasted_iota(
        jnp.int32, (QBLK, QBLK), 1
    )
    blocks = TEAM * rows // QBLK
    contract_last = (((1,), (1,)), ((), ()))

    def one_block(block, carry):
        span = pl.ds(pl.multiple_of(block * QBLK, QBLK), QBLK)
        near_key = kv_ref[span, pl.ds(0, HD)]
        near_value = kv_ref[span, pl.ds(HD, HD)]
        for head in range(query_count):
            query = q_buf[span, pl.ds(head * HD, HD)]
            at = ((query_first - 2 + head) * blocks + block) * SEL
            slots = [lists_ref[at + j] for j in range(SEL)]
            places = [jnp.maximum(slot, 0) for slot in slots]
            keys = jnp.concatenate(
                [near_key] + [cache_ref[place, :, pl.ds(0, HD)] for place in places], axis=0
            )
            values = jnp.concatenate(
                [near_value] + [cache_ref[place, :, pl.ds(HD, HD)] for place in places], axis=0
            )
            scores = (
                lax.dot_general(query, keys, contract_last, preferred_element_type=jnp.float32)
                * scale
            )
            parts = [jnp.where(causal, scores[:, :QBLK], -jnp.inf)]
            for j in range(SEL):
                part = scores[:, (j + 1) * QBLK : (j + 2) * QBLK]
                parts.append(part + jnp.where(slots[j] >= 0, 0.0, -jnp.inf))
            top = functools.reduce(jnp.maximum, parts)
            top = jnp.max(top, axis=-1, keepdims=True)
            parts = [jnp.exp(part - top) for part in parts]
            total = jnp.sum(functools.reduce(jnp.add, parts), axis=-1, keepdims=True)
            weights = jnp.concatenate([part.astype(jnp.bfloat16) for part in parts], axis=1)
            mixed = jnp.dot(weights, values, preferred_element_type=jnp.float32)
            o_buf[span, pl.ds(head * HD, HD)] = mixed / total
        return carry

    lax.fori_loop(0, blocks, one_block, 0)
    for r in range(TEAM):
        out_refs[r][...] = o_buf[pl.ds(r * rows, rows), :].astype(out_refs[r].dtype)


def heads(tiles, offsets, lists, x_parts, pieces, weights, bias, cosine, sine, cache, kv):
    first_tile, last_tile = tiles
    has_kv = first_tile == 0
    query_count = last_tile - max(first_tile, 2)
    width = (last_tile - first_tile) * HD
    rows, depth = x_parts[0].shape
    everything = TEAM * rows
    smem = pl.BlockSpec(memory_space=pltpu.SMEM)
    hbm = pl.BlockSpec(memory_space=pl.ANY)
    vmem = pl.BlockSpec(memory_space=pltpu.VMEM)
    operands, specs = [offsets], [smem]

    def add(values, spec):
        operands.extend(values)
        specs.extend([spec] * len(values))

    if query_count:
        add([lists], smem)
    add(x_parts, hbm)
    add(pieces, hbm)
    add(weights, hbm)
    add([bias, cosine, sine], vmem)
    if query_count:
        add([cache], vmem)
    if not has_kv:
        add([kv], vmem)
    shapes = []
    if has_kv:
        shapes.append(jax.ShapeDtypeStruct((rows, 2 * HD), jnp.float32))
        shapes.append(jax.ShapeDtypeStruct((everything, 2 * HD), jnp.bfloat16))
    if query_count:
        for r in range(TEAM):
            dtype = jnp.float32 if r == 0 else jnp.bfloat16
            shapes.append(jax.ShapeDtypeStruct((rows, query_count * HD), dtype))
    scratch = [
        pltpu.VMEM((everything, depth), jnp.bfloat16),
        pltpu.VMEM((depth, width), jnp.bfloat16),
        pltpu.SemaphoreType.DMA((TEAM,)),
        pltpu.SemaphoreType.DMA((len(pieces) + 3,)),
    ]
    if query_count:
        scratch.append(pltpu.VMEM((everything, query_count * HD), jnp.bfloat16))
        scratch.append(pltpu.VMEM((everything, query_count * HD), jnp.float32))
    return pl.pallas_call(
        functools.partial(heads_kernel, tiles, len(pieces), pieces[0].shape[0]),
        out_shape=shapes,
        in_specs=specs,
        out_specs=[vmem] * len(shapes),
        scratch_shapes=scratch,
        compiler_params=pltpu.CompilerParams(vmem_limit_bytes=48 * 1024 * 1024),
        cost_estimate=pl.CostEstimate(
            flops=2 * everything * depth * width,
            bytes_accessed=2 * depth * (everything + width),
            transcendentals=everything * query_count * (SEL + 1) * QBLK,
        ),
    )(*operands)


def finish_kernel(chunk_count, places_ref, *refs):
    kv_refs = refs[:TEAM]
    context_refs = refs[TEAM : TEAM + TEAM * chunk_count]
    context_ref, keys_ref, values_ref = refs[TEAM + TEAM * chunk_count :]
    for r in range(TEAM):
        place = places_ref[r]
        column = pl.ds(pl.multiple_of(place * HD, HD), HD)
        keys_ref[:, column] = kv_refs[r][:, pl.ds(0, HD)].astype(jnp.float32)
        values_ref[:, column] = kv_refs[r][:, pl.ds(HD, HD)].astype(jnp.float32)
        at = place * (GROUP * HD)
        for chunk in range(chunk_count):
            ref = context_refs[chunk * TEAM + r]
            wide = ref.shape[1]
            context_ref[:, pl.ds(pl.multiple_of(at, HD), wide)] = ref[...].astype(jnp.float32)
            at = at + wide


def finish(places, kv_parts, context_parts):
    rows = kv_parts[0].shape[0]
    vmem = pl.BlockSpec(memory_space=pltpu.VMEM)
    flat = list(kv_parts) + [part for chunk in context_parts for part in chunk]
    wide = TEAM * GROUP * HD
    return pl.pallas_call(
        functools.partial(finish_kernel, len(context_parts)),
        out_shape=[
            jax.ShapeDtypeStruct((rows, wide), jnp.float32),
            jax.ShapeDtypeStruct((rows, TEAM * HD), jnp.float32),
            jax.ShapeDtypeStruct((rows, TEAM * HD), jnp.float32),
        ],
        in_specs=[pl.BlockSpec(memory_space=pltpu.SMEM)] + [vmem] * len(flat),
        out_specs=[vmem] * 3,
        compiler_params=pltpu.CompilerParams(vmem_limit_bytes=32 * 1024 * 1024),
    )(places, *flat)


def on_device(
    tokens,
    norm_gain,
    w_query,
    w_key,
    w_value,
    b_query,
    b_key,
    b_value,
    cache_keys,
    cache_values,
    block_lists,
    start_position,
):
    rows = tokens.shape[0]
    shard = w_query.shape[0]
    ctx_size, grp_size = lax.axis_size("ctx"), lax.axis_size("grp")
    me, layer = lax.axis_index("ctx"), lax.axis_index("grp")
    group = me % TEAM
    side = me // TEAM
    sides = ctx_size // TEAM
    if (shard // sides) % 16:
        sides = 1
        side = side * 0
    piece_rows = shard // sides

    half_key = lax.dynamic_slice(w_key, (side * piece_rows, group * HD), (piece_rows, HD))
    half_value = lax.dynamic_slice(w_value, (side * piece_rows, group * HD), (piece_rows, HD))
    half_query = lax.dynamic_slice(
        w_query, (side * piece_rows, group * GROUP * HD), (piece_rows, GROUP * HD)
    )
    half = jnp.concatenate([half_key, half_value, half_query], axis=1)
    grp_bits = bits_of(grp_size, 1)
    side_bits = bits_of(ctx_size, TEAM) if sides > 1 else []
    chunk_pieces, piece_places = [], None
    for first_tile, last_tile in CHUNKS:
        held = {0: half[:, first_tile * HD : last_tile * HD]}
        for bit in grp_bits:
            for far in sorted(held):
                held[far ^ bit] = swap(held[far], "grp", bit)
        pieces = {(far, 0): held[far] for far in held if far}
        for bit in side_bits:
            for far, over in sorted(pieces):
                pieces[(far, over ^ (bit // TEAM))] = swap(pieces[(far, over)], "ctx", bit)
        order = sorted(pieces)
        chunk_pieces.append([pieces[key] for key in order])
        piece_places = order
    offsets = jnp.stack(
        [group, layer * shard]
        + [(layer ^ far) * shard + (side ^ over) * piece_rows for far, over in piece_places]
    ).astype(jnp.int32)

    widened = tokens.astype(jnp.float32)
    normed = (
        widened
        * lax.rsqrt(jnp.mean(widened * widened, axis=-1, keepdims=True) + norm_eps)
        * norm_gain.astype(jnp.float32)
    ).astype(jnp.bfloat16)
    normed_two = swap(normed, "ctx", 2)
    x_parts = [normed, swap(normed, "ctx", 1), normed_two, swap(normed_two, "ctx", 1)]

    lists_two = swap(block_lists, "ctx", 2)
    list_parts = [
        block_lists,
        swap(block_lists, "ctx", 1),
        lists_two,
        swap(lists_two, "ctx", 1),
    ]
    lists = jnp.concatenate(
        [lax.dynamic_slice_in_dim(part, group * GROUP, GROUP, 0) for part in list_parts], axis=1
    )

    prefix = cache_keys.shape[0]
    store = jnp.concatenate(
        [
            cache_keys.reshape(prefix, TEAM, HD).transpose(1, 0, 2),
            cache_values.reshape(prefix, TEAM, HD).transpose(1, 0, 2),
        ],
        axis=2,
    )[:, None]
    distances = [0]
    for bit in bits_of(ctx_size, TEAM):
        store = jnp.concatenate([store, swap(store, "ctx", bit)], axis=1)
        distances = distances + [distance ^ bit for distance in distances]
    for bit, keep in ((2, 2), (1, 1)):
        mine = (me // bit) % 2
        kept = lax.dynamic_slice_in_dim(store, mine * keep, keep, 0)
        sent = lax.dynamic_slice_in_dim(store, (1 - mine) * keep, keep, 0)
        store = jnp.concatenate([kept, swap(sent, "ctx", bit)], axis=1)
        distances = distances + [distance ^ bit for distance in distances]
    blocks_each = prefix // QBLK
    cache = store.reshape(ctx_size * blocks_each, QBLK, 2 * HD)
    place_of = np.zeros((ctx_size,), np.int32)
    place_of[np.asarray(distances)] = np.arange(ctx_size)
    owner = jnp.maximum(lists, 0) // blocks_each
    place = jnp.zeros_like(owner)
    for distance in range(ctx_size):
        place = jnp.where((owner ^ me) == distance, int(place_of[distance]), place)
    place = place * blocks_each + jnp.maximum(lists, 0) % blocks_each
    lists = jnp.where(lists >= 0, place, -1).reshape(-1).astype(jnp.int32)

    positions = jnp.concatenate(
        [
            start_position[0]
            + ((me ^ r) * grp_size + layer) * rows
            + jnp.arange(rows, dtype=jnp.int32)
            for r in range(TEAM)
        ]
    )
    cosine, sine = rope_tables(positions)
    bias = jnp.concatenate(
        [
            lax.dynamic_slice_in_dim(b_key, group * HD, HD),
            lax.dynamic_slice_in_dim(b_value, group * HD, HD),
            lax.dynamic_slice_in_dim(b_query, group * GROUP * HD, GROUP * HD),
        ]
    ).astype(jnp.float32)[None, :]

    kv, kv_parts, context_parts = None, None, []
    for tiles, pieces in zip(CHUNKS, chunk_pieces):
        first_tile, last_tile = tiles
        results = heads(
            tiles,
            offsets,
            lists,
            x_parts,
            pieces,
            (w_query, w_key, w_value),
            bias[:, first_tile * HD : last_tile * HD],
            cosine,
            sine,
            cache,
            kv,
        )
        if first_tile == 0:
            kv_own, kv = results[:2]
            results = results[2:]
            kv_parts = [kv_own] + [
                swap(kv[r * rows : (r + 1) * rows], "ctx", r) for r in range(1, TEAM)
            ]
        if results:
            context_parts.append(
                [results[0]] + [swap(results[r], "ctx", r) for r in range(1, TEAM)]
            )
    places = jnp.stack([group ^ r for r in range(TEAM)]).astype(jnp.int32)
    return tuple(finish(places, kv_parts, context_parts))


def solution(mesh):
    in_specs = (
        P(("ctx", "grp"), None),
        P(),
        P("grp", None),
        P("grp", None),
        P("grp", None),
        P(),
        P(),
        P(),
        P("ctx", None),
        P("ctx", None),
        P(None, ("ctx", "grp"), None),
        P(),
    )
    out_specs = (P(("ctx", "grp"), None), P(("ctx", "grp"), None), P(("ctx", "grp"), None))
    return jax.shard_map(
        on_device, mesh=mesh, in_specs=in_specs, out_specs=out_specs, check_vma=False
    )
```

```python
import functools

import jax
import jax.numpy as jnp
import numpy as np
from jax import lax
from jax.experimental import pallas as pl
from jax.experimental.pallas import tpu as pltpu
from jax.sharding import PartitionSpec as P

HD = 128
GROUP = 5
QBLK = 128
SEL = 4
TEAM = 4

norm_eps = 1e-06
rope_base = 10000000.0

CHUNKS = ((0, 3), (3, 5), (5, 7))

SMEM = pl.BlockSpec(memory_space=pltpu.SMEM)
VMEM = pl.BlockSpec(memory_space=pltpu.VMEM)
ANY = pl.BlockSpec(memory_space=pl.ANY)


def angle_tables(head_dim):
    half_dim = head_dim // 2
    frequency = rope_base ** (-2.0 * np.arange(half_dim) / head_dim)
    return np.stack(
        [np.mod(frequency * 32.0**digit_level, 2.0 * np.pi) for digit_level in range(4)]
    )


def rope_tables(positions):
    tables = jnp.asarray(np.tile(angle_tables(HD), (1, 2)), jnp.float32)
    angles = jnp.zeros((positions.shape[0], HD), jnp.float32)
    remaining = positions
    for digit_level in range(4):
        digit_value = (remaining % 32).astype(jnp.float32)
        angles = angles + digit_value[:, None] * tables[digit_level][None, :]
        remaining = remaining // 32
    sign = jnp.where(jnp.arange(HD) < HD // 2, -1.0, 1.0).astype(jnp.float32)
    return jnp.cos(angles), jnp.sin(angles) * sign


def swap(value, axis, bit):
    size = lax.axis_size(axis)
    return lax.ppermute(value, axis, [(i, i ^ bit) for i in range(size)])


def bits_of(size, low):
    bits = []
    bit = low
    while bit < size:
        bits.append(bit)
        bit *= 2
    return bits[::-1]


def tile_sources(first, last, group):
    parts = []
    for source in (0, 1):
        if first <= source < last:
            parts.append((source, group * HD, 1))
    query_first = max(first, 2)
    if last > query_first:
        parts.append((2, (group * GROUP + query_first - 2) * HD, last - query_first))
    return parts


def prep_kernel(piece_rows, *refs):
    place_ref, tokens_ref, gain_ref, wq_ref, wk_ref, wv_ref, ck_ref, cv_ref = refs[:8]
    normed_ref = refs[8]
    half_refs = refs[9 : 9 + len(CHUNKS)]
    kept_ref, sent_ref, sem = refs[9 + len(CHUNKS) :]
    group = place_ref[0]
    local = pl.ds(pl.multiple_of(place_ref[1], 16), piece_rows)
    copies = []
    for (first, last), half_ref in zip(CHUNKS, half_refs):
        at = 0
        for source, column, tiles in tile_sources(first, last, group):
            copies.append(
                (
                    (wk_ref, wv_ref, wq_ref)[source].at[
                        local, pl.ds(pl.multiple_of(column, HD), tiles * HD)
                    ],
                    half_ref.at[:, pl.ds(at, tiles * HD)],
                )
            )
            at += tiles * HD
    pair = group // 2
    for target, first in ((sent_ref, 1 - pair), (kept_ref, pair)):
        for core in range(2):
            column = pl.ds(pl.multiple_of((first * 2 + core) * HD, HD), HD)
            copies.append((ck_ref.at[:, column], target.at[core, :, pl.ds(0, HD)]))
            copies.append((cv_ref.at[:, column], target.at[core, :, pl.ds(HD, HD)]))
    copies = [
        pltpu.make_async_copy(source, target, sem.at[index])
        for index, (source, target) in enumerate(copies)
    ]
    for copy in copies:
        copy.start()
    widened = tokens_ref[...].astype(jnp.float32)
    normed_ref[...] = (
        widened
        * lax.rsqrt(jnp.mean(widened * widened, axis=-1, keepdims=True) + norm_eps)
        * gain_ref[...].astype(jnp.float32)
    ).astype(jnp.bfloat16)
    for copy in copies:
        copy.wait()


def prep(place, piece_rows, tokens, norm_gain, weights, caches):
    prefix = caches[0].shape[0]
    shapes = [jax.ShapeDtypeStruct(tokens.shape, jnp.bfloat16)]
    count = 8
    for first, last in CHUNKS:
        shapes.append(jax.ShapeDtypeStruct((piece_rows, (last - first) * HD), jnp.bfloat16))
        count += len(tile_sources(first, last, 0))
    shapes += [jax.ShapeDtypeStruct((2, prefix, 2 * HD), jnp.bfloat16)] * 2
    return pl.pallas_call(
        functools.partial(prep_kernel, piece_rows),
        out_shape=shapes,
        in_specs=[SMEM, VMEM, VMEM] + [ANY] * 5,
        out_specs=[VMEM] + [ANY] * (len(shapes) - 1),
        scratch_shapes=[pltpu.SemaphoreType.DMA((count,))],
        compiler_params=pltpu.CompilerParams(vmem_limit_bytes=24 * 1024 * 1024),
        name="prep",
    )(place, tokens, norm_gain[None, :], *weights, *caches)


def turned(value, cosine, sine):
    return value * cosine + pltpu.roll(value, HD // 2, 1) * sine


def heads_kernel(tiles, piece_count, piece_rows, cache_places, *refs):
    first_tile, last_tile = tiles
    has_kv = first_tile == 0
    query_first = max(first_tile, 2)
    query_count = last_tile - query_first
    refs = list(refs)

    def take(count):
        taken = refs[:count]
        del refs[:count]
        return taken

    offsets_ref, lists_ref = take(2)
    x_refs = take(TEAM)
    piece_refs = take(piece_count)
    wq_ref, wk_ref, wv_ref = take(3)
    bias_ref, cosine_ref, sine_ref = take(3)
    if has_kv:
        cache_refs = take(len(cache_places))
        kv_out_refs = take(TEAM)
        key_ref, value_t_ref, cache_key_ref, cache_value_t_ref = take(4)
    else:
        key_ref, value_t_ref, cache_key_ref, cache_value_t_ref = take(4)
    out_refs = take(TEAM)
    w_buf, w_sem = take(2)
    if has_kv:
        cache_buf, cache_sem = take(2)

    rows = x_refs[0].shape[0]
    shard = wq_ref.shape[0]
    group = offsets_ref[0]
    local = pl.ds(pl.multiple_of(offsets_ref[1], 16), shard)
    copies = []
    at = 0
    for source, column, count in tile_sources(first_tile, last_tile, group):
        copies.append(
            (
                (wk_ref, wv_ref, wq_ref)[source].at[
                    :, pl.ds(pl.multiple_of(column, HD), count * HD)
                ],
                w_buf.at[local, pl.ds(at, count * HD)],
            )
        )
        at += count * HD
    for index, piece in enumerate(piece_refs):
        start = pl.multiple_of(offsets_ref[2 + index], 16)
        copies.append((piece, w_buf.at[pl.ds(start, piece_rows), :]))
    copies = [
        pltpu.make_async_copy(source, target, w_sem.at[index])
        for index, (source, target) in enumerate(copies)
    ]
    for copy in copies:
        copy.start()
    if has_kv:
        core = group % 2
        owner = offsets_ref[2 + piece_count]
        blocks_each = cache_refs[0].shape[1] // QBLK
        cache_copies = []
        for place, cache_ref in zip(cache_places, cache_refs):
            for block in range(blocks_each):
                cache_copies.append(
                    pltpu.make_async_copy(
                        cache_ref.at[core, pl.ds(block * QBLK, QBLK), :],
                        cache_buf.at[(owner ^ place) * blocks_each + block],
                        cache_sem.at[len(cache_copies)],
                    )
                )
        for copy in cache_copies:
            copy.start()
        for copy in cache_copies:
            copy.wait()
        for block in range(blocks_each * len(cache_places)):
            cache_key_ref[block] = cache_buf[block, :, pl.ds(0, HD)]
            cache_value_t_ref[block] = cache_buf[block, :, pl.ds(HD, HD)].T
    for copy in copies:
        copy.wait()

    factor = HD ** (-0.5) * float(np.log2(np.e))
    causal = lax.broadcasted_iota(jnp.int32, (QBLK, QBLK), 0) <= lax.broadcasted_iota(
        jnp.int32, (QBLK, QBLK), 1
    )
    contract_last = (((1,), (1,)), ((), ()))
    blocks = rows // QBLK
    list_rows = blocks * SEL

    for r in range(TEAM):
        span = pl.ds(r * rows, rows)
        lin = (
            jnp.dot(x_refs[r][...], w_buf[...], preferred_element_type=jnp.float32)
            + bias_ref[...]
        )
        cosine, sine = cosine_ref[span, :], sine_ref[span, :]
        queries = []
        for tile in range(first_tile, last_tile):
            at = (tile - first_tile) * HD
            value = lin[:, at : at + HD]
            if tile != 1:
                value = turned(value, cosine, sine)
            if tile >= 2:
                queries.append(value.astype(jnp.bfloat16))
                continue
            kv_out_refs[r][:, pl.ds(at, HD)] = value.astype(kv_out_refs[r].dtype)
            if tile == 0:
                key_ref[span, :] = value.astype(jnp.bfloat16)
            else:
                value_t_ref[:, span] = value.astype(jnp.bfloat16).T
        for block in range(blocks):
            part_span = pl.ds(r * rows + block * QBLK, QBLK)
            near_key = key_ref[part_span, :]
            near_value = value_t_ref[:, part_span]
            for head in range(query_count):
                query = queries[head][block * QBLK : (block + 1) * QBLK, :]
                at = (group * GROUP + query_first - 2 + head) * list_rows + block * SEL
                slots = [lists_ref[r, at + j] for j in range(SEL)]
                places = [jnp.maximum(slot, 0) for slot in slots]
                keys = jnp.concatenate(
                    [near_key] + [cache_key_ref[place] for place in places], axis=0
                )
                values = jnp.concatenate(
                    [near_value] + [cache_value_t_ref[place] for place in places], axis=1
                )
                scores = lax.dot_general(
                    keys, query, contract_last, preferred_element_type=jnp.float32
                )
                parts = [jnp.where(causal, scores[:QBLK], -jnp.inf)]
                for j in range(SEL):
                    part = scores[(j + 1) * QBLK : (j + 2) * QBLK]
                    parts.append(part + jnp.where(slots[j] >= 0, 0.0, -jnp.inf))
                top = functools.reduce(jnp.maximum, parts)
                top = jnp.max(top, axis=0, keepdims=True) * factor
                parts = [jnp.exp2(part * factor - top) for part in parts]
                total = jnp.sum(functools.reduce(jnp.add, parts), axis=0, keepdims=True)
                weights = jnp.concatenate([part.astype(jnp.bfloat16) for part in parts], axis=0)
                mixed = jnp.dot(values, weights, preferred_element_type=jnp.float32)
                out_refs[r][pl.ds(block * QBLK, QBLK), pl.ds(head * HD, HD)] = (
                    (mixed / total).T.astype(out_refs[r].dtype)
                )


def heads(tiles, offsets, lists, x_parts, pieces, weights, bias, cosine, sine, caches, near):
    first_tile, last_tile = tiles
    has_kv = first_tile == 0
    query_count = last_tile - max(first_tile, 2)
    width = (last_tile - first_tile) * HD
    rows, depth = x_parts[0].shape
    everything = TEAM * rows
    operands, specs = [], []

    def add(values, spec):
        operands.extend(values)
        specs.extend([spec] * len(values))

    add([offsets, lists], SMEM)
    add(x_parts, VMEM)
    add(pieces, ANY)
    add(weights, ANY)
    add([bias, cosine, sine], VMEM)
    shapes, out_specs = [], []
    scratch = [
        pltpu.VMEM((depth, width), jnp.bfloat16),
        pltpu.SemaphoreType.DMA((len(pieces) + 3,)),
    ]
    cache_places = ()
    if has_kv:
        cache_places, cache_parts = zip(*caches)
        add(cache_parts, ANY)
        for r in range(TEAM):
            dtype = jnp.float32 if r == 0 else jnp.bfloat16
            shapes.append(jax.ShapeDtypeStruct((rows, 2 * HD), dtype))
        total_blocks = len(caches) * cache_parts[0].shape[1] // QBLK
        shapes.append(jax.ShapeDtypeStruct((everything, HD), jnp.bfloat16))
        shapes.append(jax.ShapeDtypeStruct((HD, everything), jnp.bfloat16))
        shapes.append(jax.ShapeDtypeStruct((total_blocks, QBLK, HD), jnp.bfloat16))
        shapes.append(jax.ShapeDtypeStruct((total_blocks, HD, QBLK), jnp.bfloat16))
        scratch.append(pltpu.VMEM((total_blocks, QBLK, 2 * HD), jnp.bfloat16))
        scratch.append(pltpu.SemaphoreType.DMA((total_blocks,)))
    else:
        add(near, VMEM)
    for r in range(TEAM):
        dtype = jnp.float32 if r == 0 else jnp.bfloat16
        shapes.append(jax.ShapeDtypeStruct((rows, query_count * HD), dtype))
    return pl.pallas_call(
        functools.partial(
            heads_kernel, tiles, len(pieces), pieces[0].shape[0], tuple(cache_places)
        ),
        out_shape=shapes,
        in_specs=specs,
        out_specs=[VMEM] * len(shapes),
        scratch_shapes=scratch,
        compiler_params=pltpu.CompilerParams(vmem_limit_bytes=32 * 1024 * 1024),
        cost_estimate=pl.CostEstimate(
            flops=2 * everything * depth * width,
            bytes_accessed=2 * depth * (everything + width),
            transcendentals=everything * query_count * (SEL + 1) * QBLK,
        ),
        name="heads",
    )(*operands)


def finish_kernel(chunk_count, places_ref, *refs):
    kv_refs = refs[:TEAM]
    context_refs = refs[TEAM : TEAM + TEAM * chunk_count]
    context_ref, keys_ref, values_ref = refs[TEAM + TEAM * chunk_count :]
    for r in range(TEAM):
        place = places_ref[0] ^ r
        column = pl.ds(pl.multiple_of(place * HD, HD), HD)
        keys_ref[:, column] = kv_refs[r][:, pl.ds(0, HD)].astype(jnp.float32)
        values_ref[:, column] = kv_refs[r][:, pl.ds(HD, HD)].astype(jnp.float32)
        at = place * (GROUP * HD)
        for chunk in range(chunk_count):
            ref = context_refs[chunk * TEAM + r]
            wide = ref.shape[1]
            context_ref[:, pl.ds(pl.multiple_of(at, HD), wide)] = ref[...].astype(jnp.float32)
            at = at + wide


def finish(places, kv_parts, context_parts):
    rows = kv_parts[0].shape[0]
    flat = list(kv_parts) + [part for chunk in context_parts for part in chunk]
    wide = TEAM * GROUP * HD
    return pl.pallas_call(
        functools.partial(finish_kernel, len(context_parts)),
        out_shape=[
            jax.ShapeDtypeStruct((rows, wide), jnp.float32),
            jax.ShapeDtypeStruct((rows, TEAM * HD), jnp.float32),
            jax.ShapeDtypeStruct((rows, TEAM * HD), jnp.float32),
        ],
        in_specs=[SMEM] + [VMEM] * len(flat),
        out_specs=[VMEM] * 3,
        compiler_params=pltpu.CompilerParams(vmem_limit_bytes=24 * 1024 * 1024),
        name="finish",
    )(places, *flat)


def on_device(
    tokens,
    norm_gain,
    w_query,
    w_key,
    w_value,
    b_query,
    b_key,
    b_value,
    cache_keys,
    cache_values,
    block_lists,
    start_position,
):
    rows = tokens.shape[0]
    shard = w_query.shape[0]
    ctx_size, grp_size = lax.axis_size("ctx"), lax.axis_size("grp")
    me, layer = lax.axis_index("ctx"), lax.axis_index("grp")
    group = me % TEAM
    sides = ctx_size // TEAM
    side = me // TEAM
    if (shard // sides) % 16:
        sides = 1
        side = side * 0
    piece_rows = shard // sides
    weights = (w_query, w_key, w_value)

    grp_bits = bits_of(grp_size, 1)
    side_bits = bits_of(ctx_size, TEAM) if sides > 1 else []
    grp_order = [0]
    for bit in grp_bits:
        grp_order += [far ^ bit for far in grp_order]
    piece_places = [(far, 0) for far in sorted(grp_order) if far]
    for bit in side_bits:
        piece_places += [(far, over ^ (bit // TEAM)) for far, over in piece_places]
    piece_places = sorted(piece_places)
    offsets = jnp.stack(
        [group, layer * shard]
        + [(layer ^ far) * shard + (side ^ over) * piece_rows for far, over in piece_places]
        + [me]
    ).astype(jnp.int32)
    place = jnp.stack([group, side * piece_rows]).astype(jnp.int32)

    normed, *rest = prep(
        place, piece_rows, tokens, norm_gain, weights, (cache_keys, cache_values)
    )
    halves, (cache_kept, cache_sent) = rest[: len(CHUNKS)], rest[len(CHUNKS) :]

    chunk_pieces = []
    for half in halves:
        held = {0: half}
        for bit in grp_bits:
            for far in sorted(held):
                held[far ^ bit] = swap(held[far], "grp", bit)
        pieces = {(far, 0): held[far] for far in held if far}
        for bit in side_bits:
            for far, over in sorted(pieces):
                pieces[(far, over ^ (bit // TEAM))] = swap(pieces[(far, over)], "ctx", bit)
        chunk_pieces.append([pieces[key] for key in piece_places])

    normed_two = swap(normed, "ctx", 2)
    x_parts = [normed, swap(normed, "ctx", 1), normed_two, swap(normed_two, "ctx", 1)]

    flat_lists = block_lists.reshape(-1)
    lists_two = swap(flat_lists, "ctx", 2)
    lists = jnp.stack(
        [flat_lists, swap(flat_lists, "ctx", 1), lists_two, swap(lists_two, "ctx", 1)]
    )

    caches = [(0, cache_kept), (2, swap(cache_sent, "ctx", 2))]
    for bit in bits_of(ctx_size, TEAM) + [1]:
        caches += [(distance ^ bit, swap(value, "ctx", bit)) for distance, value in caches]

    positions = jnp.concatenate(
        [
            start_position[0]
            + ((me ^ r) * grp_size + layer) * rows
            + jnp.arange(rows, dtype=jnp.int32)
            for r in range(TEAM)
        ]
    )
    cosine, sine = rope_tables(positions)
    bias = jnp.concatenate(
        [
            lax.dynamic_slice_in_dim(b_key, group * HD, HD),
            lax.dynamic_slice_in_dim(b_value, group * HD, HD),
            lax.dynamic_slice_in_dim(b_query, group * GROUP * HD, GROUP * HD),
        ]
    ).astype(jnp.float32)[None, :]

    near, kv_parts, context_parts = None, None, []
    for tiles, pieces in zip(CHUNKS, chunk_pieces):
        first_tile, last_tile = tiles
        results = heads(
            tiles,
            offsets,
            lists,
            x_parts,
            pieces,
            weights,
            bias[:, first_tile * HD : last_tile * HD],
            cosine,
            sine,
            caches,
            near,
        )
        if first_tile == 0:
            kv_parts = [results[0]] + [swap(results[r], "ctx", r) for r in range(1, TEAM)]
            near = results[TEAM : TEAM + 4]
            results = results[TEAM + 4 :]
        context_parts.append([results[0]] + [swap(results[r], "ctx", r) for r in range(1, TEAM)])
    return tuple(finish(place, kv_parts, context_parts))


def solution(mesh):
    in_specs = (
        P(("ctx", "grp"), None),
        P(),
        P("grp", None),
        P("grp", None),
        P("grp", None),
        P(),
        P(),
        P(),
        P("ctx", None),
        P("ctx", None),
        P(None, ("ctx", "grp"), None),
        P(),
    )
    out_specs = (P(("ctx", "grp"), None), P(("ctx", "grp"), None), P(("ctx", "grp"), None))
    return jax.shard_map(
        on_device, mesh=mesh, in_specs=in_specs, out_specs=out_specs, check_vma=False
    )
```

```python
import functools

import jax
import jax.numpy as jnp
import numpy as np
from jax import lax
from jax.experimental import pallas as pl
from jax.experimental.pallas import tpu as pltpu
from jax.sharding import PartitionSpec as P

HD = 128
GROUP = 5
QBLK = 128
SEL = 4
TEAM = 4

norm_eps = 1e-06
rope_base = 10000000.0

CHUNKS = ((0, 3), (3, 5), (5, 7))
MIB = 1024 * 1024

SMEM = pl.BlockSpec(memory_space=pltpu.SMEM)
VMEM = pl.BlockSpec(memory_space=pltpu.VMEM)
ANY = pl.BlockSpec(memory_space=pl.ANY)
NOTE_ROWS = 16


def angle_tables(head_dim):
    half_dim = head_dim // 2
    frequency = rope_base ** (-2.0 * np.arange(half_dim) / head_dim)
    return np.stack(
        [np.mod(frequency * 32.0**digit_level, 2.0 * np.pi) for digit_level in range(4)]
    )


def rope_table(positions):
    tables = jnp.asarray(np.tile(angle_tables(HD), (1, 2)), jnp.float32)
    quarter = jnp.where(jnp.arange(HD) < HD // 2, 0.0, -np.pi / 2).astype(jnp.float32)
    angles = jnp.broadcast_to(quarter[None, :], (positions.shape[0], HD))
    remaining = positions
    for digit_level in range(4):
        digit_value = (remaining % 32).astype(jnp.float32)
        angles = angles + digit_value[:, None] * tables[digit_level][None, :]
        remaining = remaining // 32
    return jnp.cos(angles)


def swap(value, axis, bit):
    size = lax.axis_size(axis)
    return lax.ppermute(value, axis, [(i, i ^ bit) for i in range(size)])


def bits_of(size, low):
    bits = []
    bit = low
    while bit < size:
        bits.append(bit)
        bit *= 2
    return bits[::-1]


def tile_sources(first, last, group):
    parts = []
    for source in (0, 1):
        if first <= source < last:
            parts.append((source, group * HD, 1))
    query_first = max(first, 2)
    if last > query_first:
        parts.append((2, (group * GROUP + query_first - 2) * HD, last - query_first))
    return parts


def start_all(copies, sem):
    copies = [
        pltpu.make_async_copy(source, target, sem.at[index])
        for index, (source, target) in enumerate(copies)
    ]
    for copy in copies:
        copy.start()
    return copies


def cut_kernel(cut_rows, *refs):
    place_ref, wq_ref, wk_ref, wv_ref = refs[:4]
    half_refs = refs[4 : 4 + len(CHUNKS)]
    sem = refs[-1]
    local = pl.ds(pl.multiple_of(place_ref[1], 16), cut_rows)
    copies = []
    for (first, last), half_ref in zip(CHUNKS, half_refs):
        at = 0
        for source, column, tiles in tile_sources(first, last, place_ref[0]):
            column = pl.ds(pl.multiple_of(column, HD), tiles * HD)
            copies.append(
                (
                    (wk_ref, wv_ref, wq_ref)[source].at[local, column],
                    half_ref.at[:, pl.ds(at, tiles * HD)],
                )
            )
            at += tiles * HD
    for copy in start_all(copies, sem):
        copy.wait()


def cut(place, cut_rows, weights):
    shapes = [
        jax.ShapeDtypeStruct((cut_rows, (last - first) * HD), jnp.bfloat16)
        for first, last in CHUNKS
    ]
    count = sum(len(tile_sources(first, last, 0)) for first, last in CHUNKS)
    return pl.pallas_call(
        functools.partial(cut_kernel, cut_rows),
        out_shape=shapes,
        in_specs=[SMEM] + [ANY] * 3,
        out_specs=[VMEM] * len(shapes),
        scratch_shapes=[pltpu.SemaphoreType.DMA((count,))],
        compiler_params=pltpu.CompilerParams(vmem_limit_bytes=60 * MIB),
        name="cut",
    )(place, *weights)


def prep_kernel(team_count, split, *refs):
    tokens_ref, gain_ref, lists_ref, ck_ref, cv_ref = refs[:5]
    normed_refs = refs[5 : 5 + split]
    payload_ref, note_wide, note, sem = refs[5 + split :]
    prefix = ck_ref.shape[0]
    copies = []
    for target in range(TEAM * team_count):
        column = pl.ds(target % TEAM * HD, HD)
        body = payload_ref.at[target, pl.ds(0, prefix), :]
        copies.append((ck_ref.at[:, column], body.at[:, pl.ds(0, HD)]))
        copies.append((cv_ref.at[:, column], body.at[:, pl.ds(HD, HD)]))
    note_wide[...] = jnp.zeros_like(note_wide)
    note_wide[0:1, 0 : lists_ref.shape[1]] = lists_ref[...].astype(jnp.float32)
    note[...] = note_wide[...].astype(jnp.bfloat16)
    for target in range(TEAM * team_count):
        copies.append((note, payload_ref.at[target, pl.ds(prefix, NOTE_ROWS), :]))
    copies = start_all(copies, sem)
    rows = tokens_ref.shape[0] // split
    for index in range(split):
        widened = tokens_ref[pl.ds(index * rows, rows), :].astype(jnp.float32)
        normed_refs[index][...] = (
            widened
            * lax.rsqrt(jnp.mean(widened * widened, axis=-1, keepdims=True) + norm_eps)
            * gain_ref[...].astype(jnp.float32)
        ).astype(jnp.bfloat16)
    for copy in copies:
        copy.wait()


def prep(split, team_count, tokens, norm_gain, lists, caches):
    prefix = caches[0].shape[0]
    rows, depth = tokens.shape
    everyone = TEAM * team_count
    shapes = [jax.ShapeDtypeStruct((rows // split, depth), jnp.bfloat16)] * split
    shapes.append(
        jax.ShapeDtypeStruct((everyone, prefix + NOTE_ROWS, 2 * HD), jnp.bfloat16)
    )
    return pl.pallas_call(
        functools.partial(prep_kernel, team_count, split),
        out_shape=shapes,
        in_specs=[VMEM] * 3 + [ANY] * 2,
        out_specs=[VMEM] * split + [ANY],
        scratch_shapes=[
            pltpu.VMEM((NOTE_ROWS, 2 * HD), jnp.float32),
            pltpu.VMEM((NOTE_ROWS, 2 * HD), jnp.bfloat16),
            pltpu.SemaphoreType.DMA((3 * everyone,)),
        ],
        compiler_params=pltpu.CompilerParams(vmem_limit_bytes=14 * MIB),
        name="prep",
    )(tokens, norm_gain[None, :], lists[None, :], *caches)


def turned(value, cosine, sine):
    return value * cosine + pltpu.roll(value, HD // 2, 1) * sine


def heads_kernel(tiles, piece_count, x_count, *refs):
    first_tile, last_tile = tiles
    has_kv = first_tile == 0
    query_first = max(first_tile, 2)
    query_count = last_tile - query_first
    refs = list(refs)

    def take(count):
        taken = refs[:count]
        del refs[:count]
        return taken

    offsets_ref, lists_ref = take(2)
    x_refs = take(x_count)
    piece_refs = take(piece_count)
    local_ref, bias_ref, table_ref = take(3)
    (cache_ref,) = take(1)
    if not has_kv:
        key_ref, value_t_ref, cache_value_t_ref = take(3)
    out_refs = take(TEAM)
    if has_kv:
        key_ref, value_t_ref, cache_value_t_ref = take(3)
    w_buf, w_sem, q_buf = take(3)

    rows = sum(x_ref.shape[0] for x_ref in x_refs) // TEAM
    group = offsets_ref[0]
    copies = []
    for index, piece in enumerate((local_ref, *piece_refs)):
        start = pl.multiple_of(offsets_ref[1 + index], 16)
        copies.append((piece, w_buf.at[pl.ds(start, piece.shape[0]), :]))
    copies = start_all(copies, w_sem)
    blocks_each = (cache_ref.shape[1] - NOTE_ROWS) // QBLK

    def cached(place):
        if blocks_each == 1:
            return place, pl.ds(0, QBLK)
        return place // blocks_each, pl.ds(pl.multiple_of(place % blocks_each * QBLK, QBLK), QBLK)

    if has_kv:
        for place in range(blocks_each * cache_ref.shape[0]):
            owner, part = cached(place)
            cache_value_t_ref[place] = cache_ref[owner, part, pl.ds(HD, HD)].T
    for copy in copies:
        copy.wait()

    factor = HD ** (-0.5) * float(np.log2(np.e))
    causal = lax.broadcasted_iota(jnp.int32, (QBLK, QBLK), 0) <= lax.broadcasted_iota(
        jnp.int32, (QBLK, QBLK), 1
    )
    contract_last = (((1,), (1,)), ((), ()))
    blocks = rows // QBLK
    list_rows = blocks * SEL

    low_half = lax.broadcasted_iota(jnp.int32, (rows, HD), 1) < HD // 2
    for r in range(TEAM):
        span = pl.ds(r * rows, rows)
        parts, at = [], 0
        for x_ref in x_refs:
            if at // rows == r:
                parts.append(x_ref[...])
            at += x_ref.shape[0]
        x = jnp.concatenate(parts, axis=0) if len(parts) > 1 else parts[0]
        lin = jnp.dot(x, w_buf[...], preferred_element_type=jnp.float32) + bias_ref[...]
        table = table_ref[span, :]
        swapped = pltpu.roll(table, HD // 2, 1)
        cosine = jnp.where(low_half, table, swapped)
        sine = jnp.where(low_half, -swapped, table)
        for tile in range(first_tile, last_tile):
            at = (tile - first_tile) * HD
            value = lin[:, at : at + HD]
            if tile != 1:
                value = turned(value, cosine, sine)
            if tile >= 2:
                q_buf[span, pl.ds((tile - query_first) * HD, HD)] = value.astype(jnp.bfloat16)
                continue
            out_refs[r][:, pl.ds(at, HD)] = value.astype(out_refs[r].dtype)
            if tile == 0:
                key_ref[span, :] = value.astype(jnp.bfloat16)
            else:
                value_t_ref[:, span] = value.astype(jnp.bfloat16).T

    def one_unit(r, block, head):
            part_span = pl.ds(r * rows + block * QBLK, QBLK)
            near_key = key_ref[part_span, :]
            near_value = value_t_ref[:, part_span]
            query = q_buf[part_span, pl.ds(head * HD, HD)]
            at = (group * GROUP + query_first - 2 + head) * list_rows + block * SEL
            slots = [lists_ref[group ^ r, at + j] for j in range(SEL)]
            places = [jnp.maximum(slot, 0) for slot in slots]
            keys = [near_key]
            for place in places:
                owner, part = cached(place)
                keys.append(cache_ref[owner, part, pl.ds(0, HD)])
            keys = jnp.concatenate(keys, axis=0)
            values = jnp.concatenate(
                [near_value] + [cache_value_t_ref[place] for place in places], axis=1
            )
            scores = lax.dot_general(
                keys, query, contract_last, preferred_element_type=jnp.float32
            )
            parts = [jnp.where(causal, scores[:QBLK], -jnp.inf)]
            for j in range(SEL):
                part = scores[(j + 1) * QBLK : (j + 2) * QBLK]
                parts.append(part + jnp.where(slots[j] >= 0, 0.0, -jnp.inf))
            top = functools.reduce(jnp.maximum, parts)
            top = jnp.max(top, axis=0, keepdims=True) * factor
            parts = [jnp.exp2(part * factor - top) for part in parts]
            total = jnp.sum(functools.reduce(jnp.add, parts), axis=0, keepdims=True)
            weights = jnp.concatenate([part.astype(jnp.bfloat16) for part in parts], axis=0)
            mixed = jnp.dot(values, weights, preferred_element_type=jnp.float32)
            return (mixed / total).T

    for r in range(TEAM):
        for block in range(blocks):
            for head in range(query_count):
                out_refs[r][pl.ds(block * QBLK, QBLK), pl.ds((query_first - first_tile + head) * HD, HD)] = one_unit(r, block, head).astype(out_refs[r].dtype)


def heads(tiles, offsets, lists, x_parts, pieces, local, bias, table, cache, near):
    first_tile, last_tile = tiles
    has_kv = first_tile == 0
    query_count = last_tile - max(first_tile, 2)
    width = (last_tile - first_tile) * HD
    depth = x_parts[0].shape[1]
    everything = sum(part.shape[0] for part in x_parts)
    rows = everything // TEAM
    operands, specs = [], []

    def add(values, spec):
        operands.extend(values)
        specs.extend([spec] * len(values))

    add([offsets, lists], SMEM)
    add(x_parts, VMEM)
    add(pieces + [local], ANY)
    add([bias, table, cache], VMEM)
    if not has_kv:
        add(near, VMEM)
    shapes = []
    for r in range(TEAM):
        dtype = jnp.float32 if r == 0 else jnp.bfloat16
        shapes.append(jax.ShapeDtypeStruct((rows, width), dtype))
    if has_kv:
        total_blocks = cache.shape[0] * (cache.shape[1] - NOTE_ROWS) // QBLK
        shapes.append(jax.ShapeDtypeStruct((everything, HD), jnp.bfloat16))
        shapes.append(jax.ShapeDtypeStruct((HD, everything), jnp.bfloat16))
        shapes.append(jax.ShapeDtypeStruct((total_blocks, HD, QBLK), jnp.bfloat16))
    scratch = [
        pltpu.VMEM((depth, width), jnp.bfloat16),
        pltpu.SemaphoreType.DMA((len(pieces) + 1,)),
        pltpu.VMEM((everything, query_count * HD), jnp.bfloat16),
    ]
    return pl.pallas_call(
        functools.partial(heads_kernel, tiles, len(pieces), len(x_parts)),
        out_shape=shapes,
        in_specs=specs,
        out_specs=[VMEM] * len(shapes),
        scratch_shapes=scratch,
        compiler_params=pltpu.CompilerParams(vmem_limit_bytes=14 * MIB),
        cost_estimate=pl.CostEstimate(
            flops=2 * everything * depth * width,
            bytes_accessed=2 * depth * (everything + width),
            transcendentals=everything * query_count * (SEL + 1) * QBLK,
        ),
        name="heads",
    )(*operands)


def finish_kernel(places_ref, *refs):
    parts = refs[: TEAM * len(CHUNKS)]
    context_ref, keys_ref, values_ref = refs[TEAM * len(CHUNKS) :]
    for index, (first, last) in enumerate(CHUNKS):
        for r in range(TEAM):
            part = parts[index * TEAM + r]
            place = places_ref[0] ^ r
            at = 0
            for source, column, tiles in tile_sources(first, last, place):
                target = (keys_ref, values_ref, context_ref)[source]
                target[:, pl.ds(pl.multiple_of(column, HD), tiles * HD)] = part[
                    :, pl.ds(at, tiles * HD)
                ].astype(jnp.float32)
                at += tiles * HD


def finish(places, parts):
    rows = parts[0].shape[0]
    return pl.pallas_call(
        finish_kernel,
        out_shape=[
            jax.ShapeDtypeStruct((rows, TEAM * GROUP * HD), jnp.float32),
            jax.ShapeDtypeStruct((rows, TEAM * HD), jnp.float32),
            jax.ShapeDtypeStruct((rows, TEAM * HD), jnp.float32),
        ],
        in_specs=[SMEM] + [VMEM] * len(parts),
        out_specs=[VMEM] * 3,
        compiler_params=pltpu.CompilerParams(vmem_limit_bytes=14 * MIB),
        name="finish",
    )(places, *parts)


def on_device(
    tokens,
    norm_gain,
    w_query,
    w_key,
    w_value,
    b_query,
    b_key,
    b_value,
    cache_keys,
    cache_values,
    block_lists,
    start_position,
):
    rows = tokens.shape[0]
    shard = w_query.shape[0]
    ctx_size, grp_size = lax.axis_size("ctx"), lax.axis_size("grp")
    me, layer = lax.axis_index("ctx"), lax.axis_index("grp")
    group = me % TEAM
    sides = ctx_size // TEAM
    side = me // TEAM
    if (shard // sides) % 16:
        sides = 1
        side = side * 0
    piece_rows = shard // sides
    weights = (w_query, w_key, w_value)

    grp_bits = bits_of(grp_size, 1)
    side_bits = bits_of(ctx_size, TEAM) if sides > 1 else []
    grp_order = [0]
    for bit in grp_bits:
        grp_order += [far ^ bit for far in grp_order]
    piece_places = [(far, 0) for far in sorted(grp_order) if far]
    for bit in side_bits:
        piece_places += [(far, over ^ (bit // TEAM)) for far, over in piece_places]
    piece_places = sorted(piece_places)
    offsets = jnp.stack(
        [group, layer * shard]
        + [(layer ^ far) * shard + (side ^ over) * piece_rows for far, over in piece_places]
    ).astype(jnp.int32)
    place = jnp.stack([group, side * piece_rows]).astype(jnp.int32)

    halves = list(cut(place, piece_rows, weights))
    tokens, halves[0] = lax.optimization_barrier((tokens, halves[0]))
    *own_x, payload = prep(
        2,
        ctx_size // TEAM,
        tokens,
        norm_gain,
        block_lists.reshape(-1),
        (cache_keys, cache_values),
    )
    locals_ = cut(jnp.stack([group, 0]).astype(jnp.int32), shard, weights)

    cache = lax.all_to_all(payload, "ctx", 0, 0)
    lists = lax.dynamic_slice(
        cache,
        (me // TEAM * TEAM, cache_keys.shape[0], 0),
        (TEAM, 1, 2 * HD),
    )[:, 0, :].astype(jnp.int32)

    positions = jnp.concatenate(
        [
            start_position[0]
            + ((me ^ r) * grp_size + layer) * rows
            + jnp.arange(rows, dtype=jnp.int32)
            for r in range(TEAM)
        ]
    )
    table = rope_table(positions)
    bias = jnp.concatenate(
        [
            lax.dynamic_slice_in_dim(b_key, group * HD, HD),
            lax.dynamic_slice_in_dim(b_value, group * HD, HD),
            lax.dynamic_slice_in_dim(b_query, group * GROUP * HD, GROUP * HD),
        ]
    ).astype(jnp.float32)[None, :]

    tie = lax.optimization_barrier
    far_x = [swap(own_x[0], "ctx", 2)]
    first = grp_bits[0]
    near, parts = None, []
    held = None
    waiting = None

    def spread(held, index):
        for bit in grp_bits[1:]:
            for far in sorted(held):
                held[far ^ bit] = swap(held[far], "grp", bit)
        pieces = {(far, 0): held[far] for far in held if far}
        for bit in side_bits:
            for far, over in sorted(pieces):
                pieces[(far, over ^ (bit // TEAM))] = swap(pieces[(far, over)], "ctx", bit)
        return [pieces[key] for key in piece_places]

    def run(index, pieces, near):
        first_tile, last_tile = CHUNKS[index]
        results = heads(
            CHUNKS[index],
            offsets,
            lists,
            list(own_x) + [swap_own[0], swap_own[1]] + far_x + near_x,
            pieces,
            locals_[index],
            bias[:, first_tile * HD : last_tile * HD],
            table,
            cache,
            near,
        )
        if index == 0:
            near = results[TEAM:]
        back = [results[0]] + [swap(results[r], "ctx", r) for r in range(1, TEAM)]
        return back, near

    swap_own = [swap(part, "ctx", 1) for part in own_x]
    held0 = {0: halves[0], first: swap(halves[0], "grp", first)}
    halves[1], held0[first], cache, far_x[0], moving, table, bias = tie(
        (halves[1], held0[first], cache, far_x[0], own_x[1], table, bias)
    )
    far_x.append(swap(moving, "ctx", 2))
    held1 = {0: halves[1], first: swap(halves[1], "grp", first)}
    pieces0 = spread(held0, 0)
    halves[2], held1[first], far_x[1] = tie((halves[2], held1[first], far_x[1]))
    near_x = [swap(part, "ctx", 1) for part in far_x]
    held2 = {0: halves[2], first: swap(halves[2], "grp", first)}
    pieces1 = spread(held1, 1)
    back0, near = run(0, pieces0, None)
    held2[first], *near = tie((held2[first], *near))
    pieces2 = spread(held2, 2)
    back1, _ = run(1, pieces1, near)
    pieces2[0], *back0 = tie((pieces2[0], *back0))
    back2, _ = run(2, pieces2, near)
    return tuple(finish(place, back0 + back1 + back2))


def solution(mesh):
    in_specs = (
        P(("ctx", "grp"), None),
        P(),
        P("grp", None),
        P("grp", None),
        P("grp", None),
        P(),
        P(),
        P(),
        P("ctx", None),
        P("ctx", None),
        P(None, ("ctx", "grp"), None),
        P(),
    )
    out_specs = (P(("ctx", "grp"), None), P(("ctx", "grp"), None), P(("ctx", "grp"), None))
    return jax.shard_map(
        on_device, mesh=mesh, in_specs=in_specs, out_specs=out_specs, check_vma=False
    )
```

```python
import functools

import jax
import jax.numpy as jnp
import numpy as np
from jax import lax
from jax.experimental import pallas as pl
from jax.experimental.pallas import tpu as pltpu
from jax.sharding import PartitionSpec as P

HD = 128
GROUP = 5
QBLK = 128
SEL = 4
TEAM = 4
FARS = (0, 2, 4, 6)

norm_eps = 1e-06
rope_base = 10000000.0

TILES = 2 + GROUP
WIDTH = TILES * HD
MIB = 1024 * 1024

SMEM = pl.BlockSpec(memory_space=pltpu.SMEM)
VMEM = pl.BlockSpec(memory_space=pltpu.VMEM)
ANY = pl.BlockSpec(memory_space=pl.ANY)
NOTE_ROWS = 16


def angle_tables(head_dim):
    half_dim = head_dim // 2
    frequency = rope_base ** (-2.0 * np.arange(half_dim) / head_dim)
    return np.stack(
        [np.mod(frequency * 32.0**digit_level, 2.0 * np.pi) for digit_level in range(4)]
    )


def rope_table(positions):
    tables = jnp.asarray(np.tile(angle_tables(HD), (1, 2)), jnp.float32)
    quarter = jnp.where(jnp.arange(HD) < HD // 2, 0.0, -np.pi / 2).astype(jnp.float32)
    angles = jnp.broadcast_to(quarter[None, :], (positions.shape[0], HD))
    remaining = positions
    for digit_level in range(4):
        digit_value = (remaining % 32).astype(jnp.float32)
        angles = angles + digit_value[:, None] * tables[digit_level][None, :]
        remaining = remaining // 32
    return jnp.cos(angles)


def swap(value, axis, bit):
    size = lax.axis_size(axis)
    return lax.ppermute(value, axis, [(i, i ^ bit) for i in range(size)])


def bits_of(size, low):
    bits = []
    bit = low
    while bit < size:
        bits.append(bit)
        bit *= 2
    return bits[::-1]


def tile_sources(group):
    return (group * HD, 1, 0), (group * HD, 1, 1), (group * GROUP * HD, GROUP, 2)


def start_all(copies, sem):
    copies = [
        pltpu.make_async_copy(source, target, sem.at[index])
        for index, (source, target) in enumerate(copies)
    ]
    for copy in copies:
        copy.start()
    return copies


def cut_kernel(place_ref, wk_ref, wv_ref, wq_ref, out_ref, sem):
    part = pl.ds(pl.multiple_of(place_ref[1], 16), out_ref.shape[0])
    copies = []
    for ref, (column, tiles, at) in zip((wk_ref, wv_ref, wq_ref), tile_sources(place_ref[0])):
        column = pl.ds(pl.multiple_of(column, HD), tiles * HD)
        copies.append((ref.at[part, column], out_ref.at[:, pl.ds(at * HD, tiles * HD)]))
    for copy in start_all(copies, sem):
        copy.wait()


def cut(place, piece_rows, weights, limit):
    return pl.pallas_call(
        cut_kernel,
        out_shape=jax.ShapeDtypeStruct((piece_rows, WIDTH), jnp.bfloat16),
        in_specs=[SMEM] + [ANY] * 3,
        out_specs=VMEM,
        scratch_shapes=[pltpu.SemaphoreType.DMA((3,))],
        compiler_params=pltpu.CompilerParams(vmem_limit_bytes=limit * MIB),
        name="cut",
    )(place, *weights)


def normed_rows(tokens, gain):
    widened = tokens.astype(jnp.float32)
    return (
        widened
        * lax.rsqrt(jnp.mean(widened * widened, axis=-1, keepdims=True) + norm_eps)
        * gain.astype(jnp.float32)
    ).astype(jnp.bfloat16)


def pack_kernel(team_count, *refs):
    lists_ref, ck_ref, cv_ref, payload_ref = refs
    prefix = ck_ref.shape[0]
    for target in range(team_count):
        column = pl.ds(target // 2 % TEAM * HD, HD)
        payload_ref[target, pl.ds(0, prefix), pl.ds(0, HD)] = ck_ref[:, column]
        payload_ref[target, pl.ds(0, prefix), pl.ds(HD, HD)] = cv_ref[:, column]
        payload_ref[target, pl.ds(prefix, NOTE_ROWS), :] = lists_ref[...]


def pack(team_count, lists, caches):
    prefix = caches[0].shape[0]
    note = jnp.pad(lists.astype(jnp.bfloat16)[None, :], ((0, NOTE_ROWS - 1), (0, 2 * HD - lists.shape[0])))
    return pl.pallas_call(
        functools.partial(pack_kernel, team_count),
        out_shape=jax.ShapeDtypeStruct(
            (team_count, prefix + NOTE_ROWS, 2 * HD), jnp.bfloat16
        ),
        in_specs=[VMEM] * 3,
        out_specs=VMEM,
        compiler_params=pltpu.CompilerParams(vmem_limit_bytes=14 * MIB),
        name="pack",
    )(note, *caches)


def turned(value, cosine, sine):
    return value * cosine + pltpu.roll(value, HD // 2, 1) * sine


def heads_kernel(far, x_count, piece_count, *refs):
    refs = list(refs)

    def take(count):
        taken = refs[:count]
        del refs[:count]
        return taken

    place_ref, lists_ref = take(2)
    x_refs = take(x_count)
    gain_ref, bias_ref, table_ref, cache_ref = take(4)
    if piece_count:
        piece_refs = take(piece_count)
        out_ref, w_ref, cache_value_t_ref = take(3)
    else:
        w_ref, cache_value_t_ref, out_ref = take(3)
    q_buf, key_buf, value_t_buf, sem = take(4)

    rows = sum(x_ref.shape[0] for x_ref in x_refs)
    group = place_ref[0]
    copies = []
    if piece_count:
        for index, piece in enumerate(piece_refs):
            start = pl.multiple_of(place_ref[2 + index], 16)
            copies.append((piece, w_ref.at[pl.ds(start, piece.shape[0]), :]))
        copies = start_all(copies, sem)
    blocks_each = (cache_ref.shape[1] - NOTE_ROWS) // QBLK

    def cached(place):
        if blocks_each == 1:
            return place, pl.ds(0, QBLK)
        return place // blocks_each, pl.ds(pl.multiple_of(place % blocks_each * QBLK, QBLK), QBLK)

    if piece_count:
        for place in range(blocks_each * cache_ref.shape[0]):
            owner, part = cached(place)
            cache_value_t_ref[place] = cache_ref[owner, part, pl.ds(HD, HD)].T
    x = [normed_rows(x_ref[...], gain_ref[...]) for x_ref in x_refs]
    x = jnp.concatenate(x, axis=0) if x_count > 1 else x[0]
    for copy in copies:
        copy.wait()

    factor = HD ** (-0.5) * float(np.log2(np.e))
    causal = lax.broadcasted_iota(jnp.int32, (QBLK, QBLK), 0) <= lax.broadcasted_iota(
        jnp.int32, (QBLK, QBLK), 1
    )
    contract_last = (((1,), (1,)), ((), ()))
    blocks = rows // QBLK

    lin = jnp.dot(x, w_ref[...], preferred_element_type=jnp.float32) + bias_ref[...]
    low_half = lax.broadcasted_iota(jnp.int32, (rows, HD), 1) < HD // 2
    table = table_ref[...]
    swapped = pltpu.roll(table, HD // 2, 1)
    cosine = jnp.where(low_half, table, swapped)
    sine = jnp.where(low_half, -swapped, table)
    for tile in range(TILES):
        value = lin[:, tile * HD : (tile + 1) * HD]
        if tile != 1:
            value = turned(value, cosine, sine)
        if tile >= 2:
            q_buf[:, pl.ds((tile - 2) * HD, HD)] = value.astype(jnp.bfloat16)
            continue
        out_ref[:, pl.ds(tile * HD, HD)] = value.astype(out_ref.dtype)
        if tile == 0:
            key_buf[...] = value.astype(jnp.bfloat16)
        else:
            value_t_buf[...] = value.astype(jnp.bfloat16).T

    owner_list = place_ref[place_ref.shape[0] - 1] ^ far
    for block in range(blocks):
        span = pl.ds(block * QBLK, QBLK)
        for head in range(GROUP):
            query = q_buf[span, pl.ds(head * HD, HD)]
            at = ((group * GROUP + head) * blocks + block) * SEL
            slots = [lists_ref[owner_list, at + j] for j in range(SEL)]
            keys = [key_buf[span, :]]
            values = [value_t_buf[:, span]]
            for slot in slots:
                place = jnp.maximum(slot, 0)
                owner, part = cached(place)
                keys.append(cache_ref[owner, part, pl.ds(0, HD)])
                values.append(cache_value_t_ref[place])
            scores = lax.dot_general(
                jnp.concatenate(keys, axis=0),
                query,
                contract_last,
                preferred_element_type=jnp.float32,
            )
            parts = [jnp.where(causal, scores[:QBLK], -jnp.inf)]
            for j in range(SEL):
                part = scores[(j + 1) * QBLK : (j + 2) * QBLK]
                parts.append(part + jnp.where(slots[j] >= 0, 0.0, -jnp.inf))
            top = functools.reduce(jnp.maximum, parts)
            top = jnp.max(top, axis=0, keepdims=True) * factor
            parts = [jnp.exp2(part * factor - top) for part in parts]
            total = jnp.sum(functools.reduce(jnp.add, parts), axis=0, keepdims=True)
            weights = jnp.concatenate([part.astype(jnp.bfloat16) for part in parts], axis=0)
            mixed = jnp.dot(
                jnp.concatenate(values, axis=1), weights, preferred_element_type=jnp.float32
            )
            out_ref[span, pl.ds((2 + head) * HD, HD)] = (mixed / total).T.astype(out_ref.dtype)


def heads(far, place, lists, x_parts, gain, bias, table, cache, pieces, kept):
    depth = x_parts[0].shape[1]
    rows = sum(part.shape[0] for part in x_parts)
    operands = [place, lists, *x_parts, gain, bias, table, cache]
    specs = [SMEM] * 2 + [VMEM] * (len(x_parts) + 4)
    shapes = [jax.ShapeDtypeStruct((rows, WIDTH), jnp.bfloat16 if far else jnp.float32)]
    if pieces:
        operands += pieces
        specs += [ANY] * len(pieces)
        total_blocks = cache.shape[0] * (cache.shape[1] - NOTE_ROWS) // QBLK
        shapes.append(jax.ShapeDtypeStruct((depth, WIDTH), jnp.bfloat16))
        shapes.append(jax.ShapeDtypeStruct((total_blocks, HD, QBLK), jnp.bfloat16))
    else:
        operands += kept
        specs += [VMEM] * 2
    return pl.pallas_call(
        functools.partial(heads_kernel, far, len(x_parts), len(pieces)),
        out_shape=shapes,
        in_specs=specs,
        out_specs=[VMEM] * len(shapes),
        scratch_shapes=[
            pltpu.VMEM((rows, GROUP * HD), jnp.bfloat16),
            pltpu.VMEM((rows, HD), jnp.bfloat16),
            pltpu.VMEM((HD, rows), jnp.bfloat16),
            pltpu.SemaphoreType.DMA((max(len(pieces), 1),)),
        ],
        compiler_params=pltpu.CompilerParams(vmem_limit_bytes=16 * MIB),
        cost_estimate=pl.CostEstimate(
            flops=2 * rows * depth * WIDTH,
            bytes_accessed=2 * depth * (rows + WIDTH),
            transcendentals=rows * GROUP * (SEL + 1) * QBLK,
        ),
        name="heads",
    )(*operands)


def finish_kernel(place_ref, *refs):
    context_ref, keys_ref, values_ref = refs[len(FARS) :]
    for far, part in zip(FARS, refs):
        sources = tile_sources(place_ref[0] ^ (far // 2))
        for target, (column, tiles, at) in zip((keys_ref, values_ref, context_ref), sources):
            target[:, pl.ds(pl.multiple_of(column, HD), tiles * HD)] = part[
                :, pl.ds(at * HD, tiles * HD)
            ].astype(jnp.float32)


def finish(place, parts):
    rows = parts[0].shape[0]
    return pl.pallas_call(
        finish_kernel,
        out_shape=[
            jax.ShapeDtypeStruct((rows, TEAM * GROUP * HD), jnp.float32),
            jax.ShapeDtypeStruct((rows, TEAM * HD), jnp.float32),
            jax.ShapeDtypeStruct((rows, TEAM * HD), jnp.float32),
        ],
        in_specs=[SMEM] + [VMEM] * len(parts),
        out_specs=[VMEM] * 3,
        compiler_params=pltpu.CompilerParams(vmem_limit_bytes=16 * MIB),
        name="finish",
    )(place, *parts)


tie = lax.optimization_barrier


def on_device(
    tokens,
    norm_gain,
    w_query,
    w_key,
    w_value,
    b_query,
    b_key,
    b_value,
    cache_keys,
    cache_values,
    block_lists,
    start_position,
):
    rows = tokens.shape[0]
    shard = w_query.shape[0]
    ctx_size, grp_size = lax.axis_size("ctx"), lax.axis_size("grp")
    me, layer = lax.axis_index("ctx"), lax.axis_index("grp")
    group = me // 2 % TEAM
    core = me % 2
    piece_rows = shard // 2

    tokens_2 = swap(tokens, "ctx", 2)
    tokens_4 = swap(tokens, "ctx", 4)

    grp_order = [0]
    for bit in bits_of(grp_size, 1):
        grp_order += [far ^ bit for far in grp_order]
    piece_places = [(far, over) for far in sorted(grp_order) if far for over in (0, 1)]
    place = jnp.stack(
        [group, core * piece_rows, layer * shard]
        + [(layer ^ far) * shard + (core ^ over) * piece_rows for far, over in piece_places]
        + [me]
    ).astype(jnp.int32)
    weights = (w_key, w_value, w_query)
    half = cut(jnp.stack([group, core * piece_rows]).astype(jnp.int32), piece_rows, weights, 60)

    payload = pack(ctx_size, block_lists.reshape(-1), (cache_keys, cache_values))
    cache = lax.all_to_all(payload, "ctx", 0, 0)
    row_ids = jnp.arange(rows, dtype=jnp.int32)
    tables = [
        rope_table(start_position[0] + ((me ^ far) * grp_size + layer) * rows + row_ids)
        for far in FARS
    ]
    bias = jnp.concatenate(
        [
            lax.dynamic_slice_in_dim(b_key, group * HD, HD),
            lax.dynamic_slice_in_dim(b_value, group * HD, HD),
            lax.dynamic_slice_in_dim(b_query, group * GROUP * HD, GROUP * HD),
        ]
    ).astype(jnp.float32)[None, :]

    held = {0: half}
    for index, bit in enumerate(bits_of(grp_size, 1)):
        for far in sorted(held):
            held[far ^ bit] = swap(held[far], "grp", bit)
        if index == 0:
            held[bit], tables, bias = tie((held[bit], tables, bias))
    whole = cut(jnp.stack([group, 0]).astype(jnp.int32), shard, weights, 14)
    pieces = [whole]
    for far, over in piece_places:
        pieces.append(swap(held[far], "ctx", 1) if over else held[far])

    half_rows = rows // 2
    tokens_6 = [
        swap(tokens_2[:half_rows], "ctx", 4),
        swap(tokens_4[half_rows:], "ctx", 2),
    ]

    lists = cache[:, cache_keys.shape[0], :].astype(jnp.int32)

    x_parts = {0: [tokens], 2: [tokens_2], 4: [tokens_4], 6: tokens_6}
    kept, parts = None, {}
    for far in (2, 4, 6, 0):
        out, *rest = heads(
            far,
            place,
            lists,
            x_parts[far],
            norm_gain[None, :],
            bias,
            tables[FARS.index(far)],
            cache,
            [] if kept else pieces,
            kept,
        )
        kept = kept or rest
        parts[far] = swap(out, "ctx", far) if far else out
    return tuple(finish(place, [parts[far] for far in FARS]))


def solution(mesh):
    in_specs = (
        P(("ctx", "grp"), None),
        P(),
        P("grp", None),
        P("grp", None),
        P("grp", None),
        P(),
        P(),
        P(),
        P("ctx", None),
        P("ctx", None),
        P(None, ("ctx", "grp"), None),
        P(),
    )
    out_specs = (P(("ctx", "grp"), None), P(("ctx", "grp"), None), P(("ctx", "grp"), None))
    return jax.shard_map(
        on_device, mesh=mesh, in_specs=in_specs, out_specs=out_specs, check_vma=False
    )
```

```python
import functools

import jax
import jax.numpy as jnp
import numpy as np
from jax import lax
from jax.experimental import pallas as pl
from jax.experimental.pallas import tpu as pltpu
from jax.sharding import PartitionSpec as P

HD = 128
GROUP = 5
QBLK = 128
SEL = 4
TEAM = 4
FARS = (0, 2, 4, 6)

norm_eps = 1e-06
rope_base = 10000000.0

TILES = 2 + GROUP
WIDTH = TILES * HD
ORDER = (6, 2, 4, 0)
MIB = 1024 * 1024

SMEM = pl.BlockSpec(memory_space=pltpu.SMEM)
VMEM = pl.BlockSpec(memory_space=pltpu.VMEM)
ANY = pl.BlockSpec(memory_space=pl.ANY)
NOTE_ROWS = 16


def angle_tables(head_dim):
    half_dim = head_dim // 2
    frequency = rope_base ** (-2.0 * np.arange(half_dim) / head_dim)
    return np.stack(
        [np.mod(frequency * 32.0**digit_level, 2.0 * np.pi) for digit_level in range(4)]
    )


def rope_table(positions):
    tables = jnp.asarray(np.tile(angle_tables(HD), (1, 2)), jnp.float32)
    quarter = jnp.where(jnp.arange(HD) < HD // 2, 0.0, -np.pi / 2).astype(jnp.float32)
    angles = jnp.broadcast_to(quarter[None, :], (positions.shape[0], HD))
    remaining = positions
    for digit_level in range(4):
        digit_value = (remaining % 32).astype(jnp.float32)
        angles = angles + digit_value[:, None] * tables[digit_level][None, :]
        remaining = remaining // 32
    return jnp.cos(angles)


def swap(value, axis, bit):
    size = lax.axis_size(axis)
    return lax.ppermute(value, axis, [(i, i ^ bit) for i in range(size)])


def bits_of(size, low):
    bits = []
    bit = low
    while bit < size:
        bits.append(bit)
        bit *= 2
    return bits[::-1]


def tile_sources(group):
    return (group * HD, 1, 0), (group * HD, 1, 1), (group * GROUP * HD, GROUP, 2)


def start_all(copies, sem):
    copies = [
        pltpu.make_async_copy(source, target, sem.at[index])
        for index, (source, target) in enumerate(copies)
    ]
    for copy in copies:
        copy.start()
    return copies


def cut_kernel(wk_ref, wv_ref, wq_ref, half_ref, whole_ref, sem):
    me = lax.axis_index("ctx")
    rows = half_ref.shape[0]
    part = pl.ds(pl.multiple_of(me % 2 * rows, 16), rows)
    copies = []
    for target, run in ((half_ref, part), (whole_ref, slice(None))):
        for ref, (column, tiles, at) in zip(
            (wk_ref, wv_ref, wq_ref), tile_sources(me // 2 % TEAM)
        ):
            column = pl.ds(pl.multiple_of(column, HD), tiles * HD)
            copies.append((ref.at[run, column], target.at[:, pl.ds(at * HD, tiles * HD)]))
    for copy in start_all(copies, sem):
        copy.wait()


def cut(weights):
    shard = weights[0].shape[0]
    return pl.pallas_call(
        cut_kernel,
        out_shape=[
            jax.ShapeDtypeStruct((rows, WIDTH), jnp.bfloat16) for rows in (shard // 2, shard)
        ],
        in_specs=[ANY] * 3,
        out_specs=[VMEM] * 2,
        scratch_shapes=[pltpu.SemaphoreType.DMA((6,))],
        compiler_params=pltpu.CompilerParams(vmem_limit_bytes=60 * MIB),
        name="cut",
    )(*weights)


def gather_kernel(count, place_ref, cache_ref, *refs):
    piece_refs = refs[:count]
    w_ref, cache_value_t_ref, sem = refs[count:]
    copies = []
    for index, piece in enumerate(piece_refs):
        start = pl.multiple_of(place_ref[1 + index], 16)
        copies.append((piece, w_ref.at[pl.ds(start, piece.shape[0]), :]))
    copies = start_all(copies, sem)
    blocks_each = (cache_ref.shape[1] - NOTE_ROWS) // QBLK
    for place in range(blocks_each * cache_ref.shape[0]):
        part = pl.ds(place % blocks_each * QBLK, QBLK)
        cache_value_t_ref[place] = cache_ref[place // blocks_each, part, pl.ds(HD, HD)].T
    for copy in copies:
        copy.wait()


def gather(place, depth, cache, pieces):
    total_blocks = cache.shape[0] * (cache.shape[1] - NOTE_ROWS) // QBLK
    return pl.pallas_call(
        functools.partial(gather_kernel, len(pieces)),
        out_shape=[
            jax.ShapeDtypeStruct((depth, WIDTH), jnp.bfloat16),
            jax.ShapeDtypeStruct((total_blocks, HD, QBLK), jnp.bfloat16),
        ],
        in_specs=[SMEM, VMEM] + [ANY] * len(pieces),
        out_specs=[VMEM] * 2,
        scratch_shapes=[pltpu.SemaphoreType.DMA((len(pieces),))],
        compiler_params=pltpu.CompilerParams(vmem_limit_bytes=16 * MIB),
        name="gather",
    )(place, cache, *pieces)


def normed_rows(tokens, gain):
    widened = tokens.astype(jnp.float32)
    return (
        widened
        * lax.rsqrt(jnp.mean(widened * widened, axis=-1, keepdims=True) + norm_eps)
        * gain.astype(jnp.float32)
    ).astype(jnp.bfloat16)


def pack_kernel(team_count, *refs):
    lists_ref, ck_ref, cv_ref, payload_ref = refs
    prefix = ck_ref.shape[0]
    for target in range(team_count):
        column = pl.ds(target % TEAM * HD, HD)
        payload_ref[target, pl.ds(0, prefix), pl.ds(0, HD)] = ck_ref[:, column]
        payload_ref[target, pl.ds(0, prefix), pl.ds(HD, HD)] = cv_ref[:, column]
        payload_ref[target, pl.ds(prefix, NOTE_ROWS), :] = lists_ref[...]


def pack(team_count, lists, caches):
    prefix = caches[0].shape[0]
    note = jnp.pad(lists.astype(jnp.bfloat16)[None, :], ((0, NOTE_ROWS - 1), (0, 2 * HD - lists.shape[0])))
    return pl.pallas_call(
        functools.partial(pack_kernel, team_count),
        out_shape=jax.ShapeDtypeStruct(
            (team_count, prefix + NOTE_ROWS, 2 * HD), jnp.bfloat16
        ),
        in_specs=[VMEM] * 3,
        out_specs=VMEM,
        compiler_params=pltpu.CompilerParams(vmem_limit_bytes=14 * MIB),
        name="pack",
    )(note, *caches)


def turned(value, cosine, sine):
    return value * cosine + pltpu.roll(value, HD // 2, 1) * sine


def heads_kernel(far, x_count, piece_count, *refs):
    refs = list(refs)

    def take(count):
        taken = refs[:count]
        del refs[:count]
        return taken

    place_ref, lists_ref = take(2)
    x_refs = take(x_count)
    gain_ref, bias_ref, table_ref, cache_ref = take(4)
    cache_value_t_ref, w_ref = take(2)
    piece_refs = take(piece_count)
    (out_ref,) = take(1)
    if piece_count:
        (w_ref,) = take(1)
    q_buf, key_buf, value_t_buf, sem = take(4)

    rows = sum(x_ref.shape[0] for x_ref in x_refs)
    group = place_ref[0]
    copies = []
    if piece_count:
        for index, piece in enumerate(piece_refs):
            start = pl.multiple_of(place_ref[place_ref.shape[0] - 3 + index], 16)
            copies.append((piece, w_ref.at[pl.ds(start, piece.shape[0]), :]))
        copies = start_all(copies, sem)
    blocks_each = (cache_ref.shape[1] - NOTE_ROWS) // QBLK

    def cached(place):
        if blocks_each == 1:
            return place, pl.ds(0, QBLK)
        return place // blocks_each, pl.ds(pl.multiple_of(place % blocks_each * QBLK, QBLK), QBLK)

    x = [normed_rows(x_ref[...], gain_ref[...]) for x_ref in x_refs]
    x = jnp.concatenate(x, axis=0) if x_count > 1 else x[0]
    for copy in copies:
        copy.wait()

    factor = HD ** (-0.5) * float(np.log2(np.e))
    causal = lax.broadcasted_iota(jnp.int32, (QBLK, QBLK), 0) <= lax.broadcasted_iota(
        jnp.int32, (QBLK, QBLK), 1
    )
    contract_last = (((1,), (1,)), ((), ()))
    blocks = rows // QBLK

    lin = jnp.dot(x, w_ref[...], preferred_element_type=jnp.float32) + bias_ref[...]
    low_half = lax.broadcasted_iota(jnp.int32, (rows, HD), 1) < HD // 2
    table = table_ref[pl.ds(FARS.index(far) * rows, rows), :]
    swapped = pltpu.roll(table, HD // 2, 1)
    cosine = jnp.where(low_half, table, swapped)
    sine = jnp.where(low_half, -swapped, table)
    for tile in range(TILES):
        value = lin[:, tile * HD : (tile + 1) * HD]
        if tile != 1:
            value = turned(value, cosine, sine)
        if tile >= 2:
            q_buf[:, pl.ds((tile - 2) * HD, HD)] = value.astype(jnp.bfloat16)
            continue
        out_ref[:, pl.ds(tile * HD, HD)] = value.astype(out_ref.dtype)
        if tile == 0:
            key_buf[...] = value.astype(jnp.bfloat16)
        else:
            value_t_buf[...] = value.astype(jnp.bfloat16).T

    owner_list = (place_ref[place_ref.shape[0] - 1] ^ far) // 2
    for block in range(blocks):
        span = pl.ds(block * QBLK, QBLK)
        for head in range(GROUP):
            query = q_buf[span, pl.ds(head * HD, HD)]
            at = ((group * GROUP + head) * blocks + block) * SEL
            slots = [lists_ref[owner_list, at + j] for j in range(SEL)]
            keys = [key_buf[span, :]]
            values = [value_t_buf[:, span]]
            for slot in slots:
                place = jnp.maximum(slot, 0)
                owner, part = cached(place)
                keys.append(cache_ref[owner, part, pl.ds(0, HD)])
                values.append(cache_value_t_ref[place])
            scores = lax.dot_general(
                jnp.concatenate(keys, axis=0),
                query,
                contract_last,
                preferred_element_type=jnp.float32,
            )
            parts = [jnp.where(causal, scores[:QBLK], -jnp.inf)]
            for j in range(SEL):
                part = scores[(j + 1) * QBLK : (j + 2) * QBLK]
                parts.append(part + jnp.where(slots[j] >= 0, 0.0, -jnp.inf))
            top = functools.reduce(jnp.maximum, parts)
            top = jnp.max(top, axis=0, keepdims=True) * factor
            parts = [jnp.exp2(part * factor - top) for part in parts]
            total = jnp.sum(functools.reduce(jnp.add, parts), axis=0, keepdims=True)
            weights = jnp.concatenate([part.astype(jnp.bfloat16) for part in parts], axis=0)
            mixed = jnp.dot(
                jnp.concatenate(values, axis=1), weights, preferred_element_type=jnp.float32
            )
            out_ref[span, pl.ds((2 + head) * HD, HD)] = (mixed / total).T.astype(out_ref.dtype)


def heads(far, place, lists, x_parts, gain, bias, table, cache, pieces, kept):
    depth = x_parts[0].shape[1]
    rows = sum(part.shape[0] for part in x_parts)
    operands = [place, lists, *x_parts, gain, bias, table, cache]
    specs = [SMEM] * 2 + [VMEM] * (len(x_parts) + 4)
    shapes = [jax.ShapeDtypeStruct((rows, WIDTH), jnp.bfloat16 if far else jnp.float32)]
    operands += kept
    specs += [VMEM] * 2
    aliases = {}
    if pieces:
        aliases = {len(operands) - 1: 1}
        operands += pieces
        specs += [ANY] * len(pieces)
        shapes.append(jax.ShapeDtypeStruct((depth, WIDTH), jnp.bfloat16))
    return pl.pallas_call(
        functools.partial(heads_kernel, far, len(x_parts), len(pieces)),
        out_shape=shapes,
        in_specs=specs,
        out_specs=[VMEM] * len(shapes),
        input_output_aliases=aliases,
        scratch_shapes=[
            pltpu.VMEM((rows, GROUP * HD), jnp.bfloat16),
            pltpu.VMEM((rows, HD), jnp.bfloat16),
            pltpu.VMEM((HD, rows), jnp.bfloat16),
            pltpu.SemaphoreType.DMA((max(len(pieces), 1),)),
        ],
        compiler_params=pltpu.CompilerParams(vmem_limit_bytes=16 * MIB),
        cost_estimate=pl.CostEstimate(flops=1, bytes_accessed=1, transcendentals=0),
        name="heads",
    )(*operands)


def finish_kernel(fars, place_ref, *refs):
    context_ref, keys_ref, values_ref = refs[-3:]
    for far, part in zip(fars, refs):
        sources = tile_sources(place_ref[0] ^ (far // 2))
        for target, (column, tiles, at) in zip((keys_ref, values_ref, context_ref), sources):
            target[:, pl.ds(pl.multiple_of(column, HD), tiles * HD)] = part[
                :, pl.ds(at * HD, tiles * HD)
            ].astype(jnp.float32)


def finish(place, parts):
    fars = tuple(parts)
    rows = parts[fars[0]].shape[0]
    return pl.pallas_call(
        functools.partial(finish_kernel, fars),
        out_shape=[
            jax.ShapeDtypeStruct((rows, TEAM * width), jnp.float32)
            for width in (GROUP * HD, HD, HD)
        ],
        in_specs=[SMEM] + [VMEM] * len(fars),
        out_specs=[VMEM] * 3,
        compiler_params=pltpu.CompilerParams(vmem_limit_bytes=16 * MIB),
        name="finish",
    )(place, *parts.values())


def last_kernel(fars, place_ref, *refs):
    count = len(fars)
    outs, wides, sem = refs[count + 3 : count + 6], refs[count + 6 : -1], refs[-1]
    copies = []
    for far, part_ref, wide in zip(fars, refs, wides):
        wide[...] = part_ref[...].astype(jnp.float32)
        for index, (column, tiles, at) in enumerate(tile_sources(place_ref[0] ^ (far // 2))):
            column = pl.ds(pl.multiple_of(column, HD), tiles * HD)
            copies.append(
                (wide.at[:, pl.ds(at * HD, tiles * HD)], outs[(1, 2, 0)[index]].at[:, column])
            )
    for copy in start_all(copies, sem):
        copy.wait()


def finish_last(place, parts, outs):
    fars = tuple(parts)
    count = len(fars)
    shape = parts[fars[0]].shape
    return pl.pallas_call(
        functools.partial(last_kernel, fars),
        out_shape=[jax.ShapeDtypeStruct(out.shape, out.dtype) for out in outs],
        in_specs=[SMEM] + [VMEM] * count + [ANY] * 3,
        out_specs=[ANY] * 3,
        input_output_aliases={1 + count + index: index for index in range(3)},
        scratch_shapes=[pltpu.VMEM(shape, jnp.float32)] * count
        + [pltpu.SemaphoreType.DMA((3 * count,))],
        compiler_params=pltpu.CompilerParams(vmem_limit_bytes=16 * MIB),
        name="finish_last",
    )(place, *parts.values(), *outs)


tie = lax.optimization_barrier


def on_device(
    tokens,
    norm_gain,
    w_query,
    w_key,
    w_value,
    b_query,
    b_key,
    b_value,
    cache_keys,
    cache_values,
    block_lists,
    start_position,
):
    rows = tokens.shape[0]
    shard = w_query.shape[0]
    ctx_size, grp_size = lax.axis_size("ctx"), lax.axis_size("grp")
    me, layer = lax.axis_index("ctx"), lax.axis_index("grp")
    group = me // 2 % TEAM
    core = me % 2
    piece_rows = shard // 2

    tokens_2 = swap(tokens, "ctx", 2)
    tokens_4 = swap(tokens, "ctx", 4)
    low, high = tokens_2[: rows // 2], tokens_4[rows // 2 :]

    grp_order = [0]
    for bit in bits_of(grp_size, 1):
        grp_order += [far ^ bit for far in grp_order]
    piece_places = [(far, over) for far in sorted(grp_order) if far for over in (0, 1)]
    place = jnp.stack(
        [group, layer * shard]
        + [(layer ^ far) * shard + (core ^ over) * piece_rows for far, over in piece_places]
        + [me]
    ).astype(jnp.int32)
    weights = (w_key, w_value, w_query)
    half, whole = cut(weights)

    payload = pack(ctx_size // 2, block_lists.reshape(-1), (cache_keys, cache_values))
    same_core = [list(range(c, ctx_size, 2)) for c in range(2)]
    cache = lax.all_to_all(payload, "ctx", 0, 0, axis_index_groups=same_core)
    row_ids = jnp.arange(rows, dtype=jnp.int32)
    tables = rope_table(
        start_position[0]
        + jnp.concatenate([((me ^ far) * grp_size + layer) * rows + row_ids for far in FARS])
    )
    bias = jnp.concatenate(
        [
            lax.dynamic_slice_in_dim(b_key, group * HD, HD),
            lax.dynamic_slice_in_dim(b_value, group * HD, HD),
            lax.dynamic_slice_in_dim(b_query, group * GROUP * HD, GROUP * HD),
        ]
    ).astype(jnp.float32)[None, :]

    held = {0: half}
    for index, bit in enumerate(bits_of(grp_size, 1)):
        for far in sorted(held):
            held[far ^ bit] = swap(held[far], "grp", bit)
        if index == 0:
            held[bit], tables, bias, cache, *_ = tie((held[bit], tables, bias, cache, low, high))
    pieces = [whole]
    for far, over in piece_places:
        pieces.append(swap(held[far], "ctx", 1) if over else held[far])

    tokens_6 = [swap(low, "ctx", 4), swap(high, "ctx", 2)]
    lists = cache[:, cache_keys.shape[0], :].astype(jnp.int32)
    blocks_each = cache_keys.shape[0] // QBLK
    owner = jnp.maximum(lists, 0) // blocks_each
    owner = ((owner ^ me) & 1) * (ctx_size // 2) + owner // 2
    lists = jnp.where(lists < 0, -1, owner * blocks_each + jnp.maximum(lists, 0) % blocks_each)
    cache = jnp.concatenate([cache, swap(cache, "ctx", 1)], axis=0)

    x_parts = {0: [tokens], 2: [tokens_2], 4: [tokens_4], 6: tokens_6}
    early, late = pieces[:-2], pieces[-2:]
    w_part, cache_value_t = gather(place, tokens.shape[1], cache, early)
    late[0], x_parts[6] = tie((late[0], tokens_6))
    kept, parts = [cache_value_t, w_part], {}
    for far in ORDER:
        out, *rest = heads(
            far,
            place,
            lists,
            x_parts[far],
            norm_gain[None, :],
            bias,
            tables,
            cache,
            late,
            kept,
        )
        if rest:
            late, kept = [], [cache_value_t, rest[0]]
        parts[far] = swap(out, "ctx", far) if far else out
    early, late = ORDER[-1:] + ORDER[:-3], ORDER[-3:-1]
    outs = finish(place, {far: parts[far] for far in early})
    return tuple(finish_last(place, {far: parts[far] for far in late}, outs))


def solution(mesh):
    in_specs = (
        P(("ctx", "grp"), None),
        P(),
        P("grp", None),
        P("grp", None),
        P("grp", None),
        P(),
        P(),
        P(),
        P("ctx", None),
        P("ctx", None),
        P(None, ("ctx", "grp"), None),
        P(),
    )
    out_specs = (P(("ctx", "grp"), None), P(("ctx", "grp"), None), P(("ctx", "grp"), None))
    return jax.shard_map(
        on_device, mesh=mesh, in_specs=in_specs, out_specs=out_specs, check_vma=False
    )
```

```python
import functools

import jax
import jax.numpy as jnp
import numpy as np
from jax import lax
from jax.experimental import pallas as pl
from jax.experimental.pallas import tpu as pltpu
from jax.sharding import PartitionSpec as P

HD = 128
GROUP = 5
QBLK = 128
SEL = 4
TEAM = 4
FARS = (0, 2, 4, 6)

norm_eps = 1e-06
rope_base = 10000000.0

TILES = 2 + GROUP
WIDTH = TILES * HD
MIB = 1024 * 1024

SMEM = pl.BlockSpec(memory_space=pltpu.SMEM)
VMEM = pl.BlockSpec(memory_space=pltpu.VMEM)
ANY = pl.BlockSpec(memory_space=pl.ANY)
NOTE_ROWS = 16


def angle_tables(head_dim):
    half_dim = head_dim // 2
    frequency = rope_base ** (-2.0 * np.arange(half_dim) / head_dim)
    return np.stack(
        [np.mod(frequency * 32.0**digit_level, 2.0 * np.pi) for digit_level in range(4)]
    )


def rope_table(positions):
    tables = jnp.asarray(np.tile(angle_tables(HD), (1, 2)), jnp.float32)
    quarter = jnp.where(jnp.arange(HD) < HD // 2, 0.0, -np.pi / 2).astype(jnp.float32)
    angles = jnp.broadcast_to(quarter[None, :], (positions.shape[0], HD))
    remaining = positions
    for digit_level in range(4):
        digit_value = (remaining % 32).astype(jnp.float32)
        angles = angles + digit_value[:, None] * tables[digit_level][None, :]
        remaining = remaining // 32
    return jnp.cos(angles)


def swap(value, axis, bit):
    size = lax.axis_size(axis)
    return lax.ppermute(value, axis, [(i, i ^ bit) for i in range(size)])


def bits_of(size, low):
    bits = []
    bit = low
    while bit < size:
        bits.append(bit)
        bit *= 2
    return bits[::-1]


def tile_sources(group):
    return (group * HD, 1, 0), (group * HD, 1, 1), (group * GROUP * HD, GROUP, 2)


def start_all(copies, sem):
    copies = [
        pltpu.make_async_copy(source, target, sem.at[index])
        for index, (source, target) in enumerate(copies)
    ]
    for copy in copies:
        copy.start()
    return copies


def cut_kernel(wk_ref, wv_ref, wq_ref, half_ref, whole_ref, sem):
    me = lax.axis_index("ctx")
    rows = half_ref.shape[0]
    part = pl.ds(pl.multiple_of(me % 2 * rows, 16), rows)
    copies = []
    for target, run in ((half_ref, part), (whole_ref, slice(None))):
        for ref, (column, tiles, at) in zip(
            (wk_ref, wv_ref, wq_ref), tile_sources(me // 2 % TEAM)
        ):
            column = pl.ds(pl.multiple_of(column, HD), tiles * HD)
            copies.append((ref.at[run, column], target.at[:, pl.ds(at * HD, tiles * HD)]))
    for copy in start_all(copies, sem):
        copy.wait()


def cut(weights):
    shard = weights[0].shape[0]
    return pl.pallas_call(
        cut_kernel,
        out_shape=[
            jax.ShapeDtypeStruct((rows, WIDTH), jnp.bfloat16) for rows in (shard // 2, shard)
        ],
        in_specs=[ANY] * 3,
        out_specs=[VMEM] * 2,
        scratch_shapes=[pltpu.SemaphoreType.DMA((6,))],
        compiler_params=pltpu.CompilerParams(vmem_limit_bytes=60 * MIB),
        name="cut",
    )(*weights)


def gather_kernel(count, place_ref, cache_ref, *refs):
    piece_refs = refs[:count]
    w_ref, cache_value_t_ref, sem = refs[count:]
    copies = []
    for index, piece in enumerate(piece_refs):
        start = pl.multiple_of(place_ref[1 + index], 16)
        copies.append((piece, w_ref.at[pl.ds(start, piece.shape[0]), :]))
    copies = start_all(copies, sem)
    blocks_each = (cache_ref.shape[1] - NOTE_ROWS) // QBLK
    for place in range(blocks_each * cache_ref.shape[0]):
        part = pl.ds(place % blocks_each * QBLK, QBLK)
        cache_value_t_ref[place] = cache_ref[place // blocks_each, part, pl.ds(HD, HD)].T
    for copy in copies:
        copy.wait()


def gather(place, depth, cache, pieces):
    total_blocks = cache.shape[0] * (cache.shape[1] - NOTE_ROWS) // QBLK
    return pl.pallas_call(
        functools.partial(gather_kernel, len(pieces)),
        out_shape=[
            jax.ShapeDtypeStruct((depth, WIDTH), jnp.bfloat16),
            jax.ShapeDtypeStruct((total_blocks, HD, QBLK), jnp.bfloat16),
        ],
        in_specs=[SMEM, VMEM] + [ANY] * len(pieces),
        out_specs=[VMEM] * 2,
        scratch_shapes=[pltpu.SemaphoreType.DMA((len(pieces),))],
        compiler_params=pltpu.CompilerParams(vmem_limit_bytes=16 * MIB),
        name="gather",
    )(place, cache, *pieces)


def normed_rows(tokens, gain):
    widened = tokens.astype(jnp.float32)
    return (
        widened
        * lax.rsqrt(jnp.mean(widened * widened, axis=-1, keepdims=True) + norm_eps)
        * gain.astype(jnp.float32)
    ).astype(jnp.bfloat16)


def norm_kernel(gain_ref, *refs):
    count = len(refs) // 2
    for token_ref, normed_ref in zip(refs[:count], refs[count:]):
        normed_ref[...] = normed_rows(token_ref[...], gain_ref[...])


def norm(gain, parts):
    return pl.pallas_call(
        norm_kernel,
        out_shape=[jax.ShapeDtypeStruct(part.shape, part.dtype) for part in parts],
        in_specs=[VMEM] * (1 + len(parts)),
        out_specs=[VMEM] * len(parts),
        compiler_params=pltpu.CompilerParams(vmem_limit_bytes=20 * MIB),
        name="norm",
    )(gain, *parts)


def pack_kernel(team_count, *refs):
    lists_ref, ck_ref, cv_ref, payload_ref = refs
    prefix = ck_ref.shape[0]
    for target in range(team_count):
        column = pl.ds(target % TEAM * HD, HD)
        payload_ref[target, pl.ds(0, prefix), pl.ds(0, HD)] = ck_ref[:, column]
        payload_ref[target, pl.ds(0, prefix), pl.ds(HD, HD)] = cv_ref[:, column]
        payload_ref[target, pl.ds(prefix, NOTE_ROWS), :] = lists_ref[...]


def pack(team_count, lists, caches):
    prefix = caches[0].shape[0]
    note = jnp.pad(lists.astype(jnp.bfloat16)[None, :], ((0, NOTE_ROWS - 1), (0, 2 * HD - lists.shape[0])))
    return pl.pallas_call(
        functools.partial(pack_kernel, team_count),
        out_shape=jax.ShapeDtypeStruct(
            (team_count, prefix + NOTE_ROWS, 2 * HD), jnp.bfloat16
        ),
        in_specs=[VMEM] * 3,
        out_specs=VMEM,
        compiler_params=pltpu.CompilerParams(vmem_limit_bytes=14 * MIB),
        name="pack",
    )(note, *caches)


def turned(value, cosine, sine):
    return value * cosine + pltpu.roll(value, HD // 2, 1) * sine


def heads_kernel(far, first_row, x_count, piece_count, *refs):
    refs = list(refs)

    def take(count):
        taken = refs[:count]
        del refs[:count]
        return taken

    place_ref, lists_ref = take(2)
    x_refs = take(x_count)
    gain_ref, bias_ref, table_ref, cache_ref = take(4)
    cache_value_t_ref, w_ref = take(2)
    piece_refs = take(piece_count)
    (out_ref,) = take(1)
    if piece_count:
        (w_ref,) = take(1)
    q_buf, key_buf, value_t_buf, sem = take(4)

    rows = sum(x_ref.shape[0] for x_ref in x_refs)
    group = place_ref[0]
    copies = []
    if piece_count:
        for index, piece in enumerate(piece_refs):
            start = pl.multiple_of(place_ref[place_ref.shape[0] - 3 + index], 16)
            copies.append((piece, w_ref.at[pl.ds(start, piece.shape[0]), :]))
        copies = start_all(copies, sem)
    blocks_each = (cache_ref.shape[1] - NOTE_ROWS) // QBLK

    def cached(place):
        if blocks_each == 1:
            return place, pl.ds(0, QBLK)
        return place // blocks_each, pl.ds(pl.multiple_of(place % blocks_each * QBLK, QBLK), QBLK)

    if far == FARS[-1]:
        x = [normed_rows(x_ref[...], gain_ref[...]) for x_ref in x_refs]
    else:
        x = [x_ref[...] for x_ref in x_refs]
    x = jnp.concatenate(x, axis=0) if x_count > 1 else x[0]
    for copy in copies:
        copy.wait()

    factor = HD ** (-0.5) * float(np.log2(np.e))
    causal = lax.broadcasted_iota(jnp.int32, (QBLK, QBLK), 0) <= lax.broadcasted_iota(
        jnp.int32, (QBLK, QBLK), 1
    )
    contract_last = (((1,), (1,)), ((), ()))
    blocks = rows // QBLK

    lin = jnp.dot(x, w_ref[...], preferred_element_type=jnp.float32) + bias_ref[...]
    low_half = lax.broadcasted_iota(jnp.int32, (rows, HD), 1) < HD // 2
    all_rows = table_ref.shape[0] // len(FARS)
    table = table_ref[pl.ds(FARS.index(far) * all_rows + first_row, rows), :]
    swapped = pltpu.roll(table, HD // 2, 1)
    cosine = jnp.where(low_half, table, swapped)
    sine = jnp.where(low_half, -swapped, table)
    for tile in range(TILES):
        value = lin[:, tile * HD : (tile + 1) * HD]
        if tile != 1:
            value = turned(value, cosine, sine)
        if tile >= 2:
            q_buf[:, pl.ds((tile - 2) * HD, HD)] = value.astype(jnp.bfloat16)
            continue
        out_ref[:, pl.ds(tile * HD, HD)] = value.astype(out_ref.dtype)
        if tile == 0:
            key_buf[...] = value.astype(jnp.bfloat16)
        else:
            value_t_buf[...] = value.astype(jnp.bfloat16).T

    owner_list = (place_ref[place_ref.shape[0] - 1] ^ far) // 2
    for block in range(blocks):
        span = pl.ds(block * QBLK, QBLK)
        for head in range(GROUP):
            query = q_buf[span, pl.ds(head * HD, HD)]
            listed = (group * GROUP + head) * (all_rows // QBLK) + first_row // QBLK + block
            at = listed * SEL
            slots = [lists_ref[owner_list, at + j] for j in range(SEL)]
            keys = [key_buf[span, :]]
            values = [value_t_buf[:, span]]
            for slot in slots:
                place = jnp.maximum(slot, 0)
                owner, part = cached(place)
                keys.append(cache_ref[owner, part, pl.ds(0, HD)])
                values.append(cache_value_t_ref[place])
            scores = lax.dot_general(
                jnp.concatenate(keys, axis=0),
                query,
                contract_last,
                preferred_element_type=jnp.float32,
            )
            parts = [jnp.where(causal, scores[:QBLK], -jnp.inf)]
            for j in range(SEL):
                part = scores[(j + 1) * QBLK : (j + 2) * QBLK]
                parts.append(part + jnp.where(slots[j] >= 0, 0.0, -jnp.inf))
            top = functools.reduce(jnp.maximum, parts)
            top = jnp.max(top, axis=0, keepdims=True) * factor
            parts = [jnp.exp2(part * factor - top) for part in parts]
            total = jnp.sum(functools.reduce(jnp.add, parts), axis=0, keepdims=True)
            weights = jnp.concatenate([part.astype(jnp.bfloat16) for part in parts], axis=0)
            mixed = jnp.dot(
                jnp.concatenate(values, axis=1), weights, preferred_element_type=jnp.float32
            )
            out_ref[span, pl.ds((2 + head) * HD, HD)] = (mixed / total).T.astype(out_ref.dtype)


def heads(far, first_row, place, lists, x_parts, gain, bias, table, cache, pieces, kept):
    depth = x_parts[0].shape[1]
    rows = sum(part.shape[0] for part in x_parts)
    operands = [place, lists, *x_parts, gain, bias, table, cache]
    specs = [SMEM] * 2 + [VMEM] * (len(x_parts) + 4)
    shapes = [jax.ShapeDtypeStruct((rows, WIDTH), jnp.bfloat16 if far else jnp.float32)]
    operands += kept
    specs += [VMEM] * 2
    aliases = {}
    if pieces:
        aliases = {len(operands) - 1: 1}
        operands += pieces
        specs += [ANY] * len(pieces)
        shapes.append(jax.ShapeDtypeStruct((depth, WIDTH), jnp.bfloat16))
    return pl.pallas_call(
        functools.partial(heads_kernel, far, first_row, len(x_parts), len(pieces)),
        out_shape=shapes,
        in_specs=specs,
        out_specs=[VMEM] * len(shapes),
        input_output_aliases=aliases,
        scratch_shapes=[
            pltpu.VMEM((rows, GROUP * HD), jnp.bfloat16),
            pltpu.VMEM((rows, HD), jnp.bfloat16),
            pltpu.VMEM((HD, rows), jnp.bfloat16),
            pltpu.SemaphoreType.DMA((max(len(pieces), 1),)),
        ],
        compiler_params=pltpu.CompilerParams(vmem_limit_bytes=16 * MIB),
        cost_estimate=pl.CostEstimate(flops=1, bytes_accessed=1, transcendentals=0),
        name="heads",
    )(*operands)


def finish_kernel(runs, place_ref, *refs):
    context_ref, keys_ref, values_ref = refs[-3:]
    for (far, first_row), part in zip(runs, refs):
        rows = pl.ds(first_row, part.shape[0])
        sources = tile_sources(place_ref[0] ^ (far // 2))
        for target, (column, tiles, at) in zip((keys_ref, values_ref, context_ref), sources):
            target[rows, pl.ds(pl.multiple_of(column, HD), tiles * HD)] = part[
                :, pl.ds(at * HD, tiles * HD)
            ].astype(jnp.float32)


def finish(place, rows, parts):
    return pl.pallas_call(
        functools.partial(finish_kernel, tuple(parts)),
        out_shape=[
            jax.ShapeDtypeStruct((rows, TEAM * width), jnp.float32)
            for width in (GROUP * HD, HD, HD)
        ],
        in_specs=[SMEM] + [VMEM] * len(parts),
        out_specs=[VMEM] * 3,
        compiler_params=pltpu.CompilerParams(vmem_limit_bytes=16 * MIB),
        name="finish",
    )(place, *parts.values())


def last_kernel(runs, place_ref, *refs):
    count = len(runs)
    outs, wides, sem = refs[count + 3 : count + 6], refs[count + 6 : -1], refs[-1]
    copies = []
    for (far, first_row), part_ref, wide in zip(runs, refs, wides):
        rows = pl.ds(first_row, part_ref.shape[0])
        for index, (column, tiles, at) in enumerate(tile_sources(place_ref[0] ^ (far // 2))):
            span = pl.ds(at * HD, tiles * HD)
            wide[:, span] = part_ref[:, span].astype(jnp.float32)
            column = pl.ds(pl.multiple_of(column, HD), tiles * HD)
            copy = pltpu.make_async_copy(
                wide.at[:, span], outs[(1, 2, 0)[index]].at[rows, column], sem.at[len(copies)]
            )
            copy.start()
            copies.append(copy)
    for copy in copies:
        copy.wait()


def finish_last(place, parts, outs):
    count = len(parts)
    return pl.pallas_call(
        functools.partial(last_kernel, tuple(parts)),
        out_shape=[jax.ShapeDtypeStruct(out.shape, out.dtype) for out in outs],
        in_specs=[SMEM] + [VMEM] * count + [ANY] * 3,
        out_specs=[ANY] * 3,
        input_output_aliases={1 + count + index: index for index in range(3)},
        scratch_shapes=[pltpu.VMEM(part.shape, jnp.float32) for part in parts.values()]
        + [pltpu.SemaphoreType.DMA((3 * count,))],
        compiler_params=pltpu.CompilerParams(vmem_limit_bytes=16 * MIB),
        name="finish_last",
    )(place, *parts.values(), *outs)


tie = lax.optimization_barrier


def on_device(
    tokens,
    norm_gain,
    w_query,
    w_key,
    w_value,
    b_query,
    b_key,
    b_value,
    cache_keys,
    cache_values,
    block_lists,
    start_position,
):
    rows = tokens.shape[0]
    shard = w_query.shape[0]
    ctx_size, grp_size = lax.axis_size("ctx"), lax.axis_size("grp")
    me, layer = lax.axis_index("ctx"), lax.axis_index("grp")
    group = me // 2 % TEAM
    core = me % 2
    piece_rows = shard // 2

    tokens_2 = swap(tokens, "ctx", 2)
    tokens_4 = swap(tokens, "ctx", 4)
    low, high = tokens_2[: rows // 2], tokens_4[rows // 2 :]

    grp_order = [0]
    for bit in bits_of(grp_size, 1):
        grp_order += [far ^ bit for far in grp_order]
    piece_places = [(far, over) for far in sorted(grp_order) if far for over in (0, 1)]
    place = jnp.stack(
        [group, layer * shard]
        + [(layer ^ far) * shard + (core ^ over) * piece_rows for far, over in piece_places]
        + [me]
    ).astype(jnp.int32)
    weights = (w_key, w_value, w_query)
    half, whole = cut(weights)

    payload = pack(ctx_size // 2, block_lists.reshape(-1), (cache_keys, cache_values))
    same_core = [list(range(c, ctx_size, 2)) for c in range(2)]
    cache = lax.all_to_all(payload, "ctx", 0, 0, axis_index_groups=same_core)
    row_ids = jnp.arange(rows, dtype=jnp.int32)
    tables = rope_table(
        start_position[0]
        + jnp.concatenate([((me ^ far) * grp_size + layer) * rows + row_ids for far in FARS])
    )
    bias = jnp.concatenate(
        [
            lax.dynamic_slice_in_dim(b_key, group * HD, HD),
            lax.dynamic_slice_in_dim(b_value, group * HD, HD),
            lax.dynamic_slice_in_dim(b_query, group * GROUP * HD, GROUP * HD),
        ]
    ).astype(jnp.float32)[None, :]

    tokens_6 = [swap(low, "ctx", 4), swap(high, "ctx", 2)]
    held = {0: half}
    for index, bit in enumerate(bits_of(grp_size, 1)):
        for far in sorted(held):
            held[far ^ bit] = swap(held[far], "grp", bit)
        if index == 0:
            held[bit], tables, bias, cache, *_ = tie((held[bit], tables, bias, cache, low, high))
    lists = cache[:, cache_keys.shape[0], :].astype(jnp.int32)
    blocks_each = cache_keys.shape[0] // QBLK
    owner = jnp.maximum(lists, 0) // blocks_each
    owner = ((owner ^ me) & 1) * (ctx_size // 2) + owner // 2
    lists = jnp.where(lists < 0, -1, owner * blocks_each + jnp.maximum(lists, 0) % blocks_each)
    cache = jnp.concatenate([cache, swap(cache, "ctx", 1)], axis=0)
    last_far = max(held)
    normed = norm(norm_gain[None, :], [tokens_2, tokens_4, tokens])
    held[last_far], *_ = tie((held[last_far], *tokens_6, cache, *normed))
    pieces = [whole]
    for far, over in piece_places:
        pieces.append(swap(held[far], "ctx", 1) if over else held[far])


    early, late = pieces[:-2], pieces[-2:]
    w_part, cache_value_t = gather(place, tokens.shape[1], cache, early)
    late[0], tokens_6 = tie((late[0], tokens_6))
    runs = {
        (6, 0): tokens_6,
        (2, 0): normed[0],
        (4, 0): normed[1],
        (0, 0): normed[2],
    }
    kept, parts = [cache_value_t, w_part], {}
    for (far, first_row), x in runs.items():
        out, *rest = heads(
            far,
            first_row,
            place,
            lists,
            x if far == 6 else [x],
            norm_gain[None, :],
            bias,
            tables,
            cache,
            late,
            kept,
        )
        if rest:
            late, kept = [], [cache_value_t, rest[0]]
        parts[(far, first_row)] = swap(out, "ctx", far) if far else out
    first = {run: parts[run] for run in parts if run[0] in (0, 6)}
    last = {run: parts[run] for run in parts if run[0] in (2, 4)}
    return tuple(finish_last(place, last, finish(place, rows, first)))


def solution(mesh):
    in_specs = (
        P(("ctx", "grp"), None),
        P(),
        P("grp", None),
        P("grp", None),
        P("grp", None),
        P(),
        P(),
        P(),
        P("ctx", None),
        P("ctx", None),
        P(None, ("ctx", "grp"), None),
        P(),
    )
    out_specs = (P(("ctx", "grp"), None), P(("ctx", "grp"), None), P(("ctx", "grp"), None))
    return jax.shard_map(
        on_device, mesh=mesh, in_specs=in_specs, out_specs=out_specs, check_vma=False
    )
```

```python
import functools

import jax
import jax.numpy as jnp
import numpy as np
from jax import lax
from jax.experimental import pallas as pl
from jax.experimental.pallas import tpu as pltpu
from jax.sharding import PartitionSpec as P

HD = 128
GROUP = 5
QBLK = 128
SEL = 4
TEAM = 4
FARS = (0, 2, 4, 6)

norm_eps = 1e-06
rope_base = 10000000.0

TILES = 2 + GROUP
WIDTH = TILES * HD
MIB = 1024 * 1024

SMEM = pl.BlockSpec(memory_space=pltpu.SMEM)
VMEM = pl.BlockSpec(memory_space=pltpu.VMEM)
ANY = pl.BlockSpec(memory_space=pl.ANY)
NOTE_ROWS = 16


def angle_tables(head_dim):
    half_dim = head_dim // 2
    frequency = rope_base ** (-2.0 * np.arange(half_dim) / head_dim)
    return np.stack(
        [np.mod(frequency * 32.0**digit_level, 2.0 * np.pi) for digit_level in range(4)]
    )


def rope_table(positions):
    tables = jnp.asarray(np.tile(angle_tables(HD), (1, 2)), jnp.float32)
    quarter = jnp.where(jnp.arange(HD) < HD // 2, 0.0, -np.pi / 2).astype(jnp.float32)
    angles = jnp.broadcast_to(quarter[None, :], (positions.shape[0], HD))
    remaining = positions
    for digit_level in range(4):
        digit_value = (remaining % 32).astype(jnp.float32)
        angles = angles + digit_value[:, None] * tables[digit_level][None, :]
        remaining = remaining // 32
    return jnp.cos(angles)


def swap(value, axis, bit):
    size = lax.axis_size(axis)
    return lax.ppermute(value, axis, [(i, i ^ bit) for i in range(size)])


def bits_of(size, low):
    bits = []
    bit = low
    while bit < size:
        bits.append(bit)
        bit *= 2
    return bits[::-1]


def tile_sources(group):
    return (group * HD, 1, 0), (group * HD, 1, 1), (group * GROUP * HD, GROUP, 2)


def start_all(copies, sem):
    copies = [
        pltpu.make_async_copy(source, target, sem.at[index])
        for index, (source, target) in enumerate(copies)
    ]
    for copy in copies:
        copy.start()
    return copies


def cut_kernel(wk_ref, wv_ref, wq_ref, half_ref, whole_ref, sem):
    me = lax.axis_index("ctx")
    rows = half_ref.shape[0]
    part = pl.ds(pl.multiple_of(me % 2 * rows, 16), rows)
    copies = []
    for target, run in ((half_ref, part), (whole_ref, slice(None))):
        for ref, (column, tiles, at) in zip(
            (wk_ref, wv_ref, wq_ref), tile_sources(me // 2 % TEAM)
        ):
            column = pl.ds(pl.multiple_of(column, HD), tiles * HD)
            copies.append((ref.at[run, column], target.at[:, pl.ds(at * HD, tiles * HD)]))
    for copy in start_all(copies, sem):
        copy.wait()


def cut(weights):
    shard = weights[0].shape[0]
    return pl.pallas_call(
        cut_kernel,
        out_shape=[
            jax.ShapeDtypeStruct((rows, WIDTH), jnp.bfloat16) for rows in (shard // 2, shard)
        ],
        in_specs=[ANY] * 3,
        out_specs=[VMEM] * 2,
        scratch_shapes=[pltpu.SemaphoreType.DMA((6,))],
        compiler_params=pltpu.CompilerParams(vmem_limit_bytes=60 * MIB),
        name="cut",
    )(*weights)


def gather_kernel(count, place_ref, cache_ref, gain_ref, *refs):
    piece_refs = refs[:count]
    x_refs = refs[count:-5]
    w_ref, cache_value_t_ref, normed_ref, x_buf, sem = refs[-5:]
    copies, first_row = [], 0
    for x_ref in x_refs:
        copies.append((x_ref, x_buf.at[pl.ds(first_row, x_ref.shape[0]), :]))
        first_row += x_ref.shape[0]
    for index, piece in enumerate(piece_refs):
        start = pl.multiple_of(place_ref[1 + index], 16)
        copies.append((piece, w_ref.at[pl.ds(start, piece.shape[0]), :]))
    copies = start_all(copies, sem)
    blocks_each = (cache_ref.shape[1] - NOTE_ROWS) // QBLK
    for place in range(blocks_each * cache_ref.shape[0]):
        part = pl.ds(place % blocks_each * QBLK, QBLK)
        cache_value_t_ref[place] = cache_ref[place // blocks_each, part, pl.ds(HD, HD)].T
    for copy in copies[: len(x_refs)]:
        copy.wait()
    normed_ref[...] = normed_rows(x_buf[...], gain_ref[...])
    for copy in copies[len(x_refs) :]:
        copy.wait()


def gather(place, gain, cache, pieces, x_parts):
    depth = x_parts[0].shape[1]
    rows = sum(part.shape[0] for part in x_parts)
    total_blocks = cache.shape[0] * (cache.shape[1] - NOTE_ROWS) // QBLK
    return pl.pallas_call(
        functools.partial(gather_kernel, len(pieces)),
        out_shape=[
            jax.ShapeDtypeStruct((depth, WIDTH), jnp.bfloat16),
            jax.ShapeDtypeStruct((total_blocks, HD, QBLK), jnp.bfloat16),
            jax.ShapeDtypeStruct((rows, depth), jnp.bfloat16),
        ],
        in_specs=[SMEM, VMEM, VMEM] + [ANY] * (len(pieces) + len(x_parts)),
        out_specs=[VMEM] * 3,
        scratch_shapes=[
            pltpu.VMEM((rows, depth), jnp.bfloat16),
            pltpu.SemaphoreType.DMA((len(pieces) + len(x_parts),)),
        ],
        compiler_params=pltpu.CompilerParams(vmem_limit_bytes=16 * MIB),
        name="gather",
    )(place, cache, gain, *pieces, *x_parts)


def normed_rows(tokens, gain):
    widened = tokens.astype(jnp.float32)
    return (
        widened
        * lax.rsqrt(jnp.mean(widened * widened, axis=-1, keepdims=True) + norm_eps)
        * gain.astype(jnp.float32)
    ).astype(jnp.bfloat16)


def norm_kernel(gain_ref, *refs):
    count = len(refs) // 2
    for token_ref, normed_ref in zip(refs[:count], refs[count:]):
        normed_ref[...] = normed_rows(token_ref[...], gain_ref[...])


def norm(gain, parts):
    return pl.pallas_call(
        norm_kernel,
        out_shape=[jax.ShapeDtypeStruct(part.shape, part.dtype) for part in parts],
        in_specs=[VMEM] * (1 + len(parts)),
        out_specs=[VMEM] * len(parts),
        compiler_params=pltpu.CompilerParams(vmem_limit_bytes=20 * MIB),
        name="norm",
    )(gain, *parts)


def pack_kernel(team_count, *refs):
    lists_ref, ck_ref, cv_ref, payload_ref = refs
    prefix = ck_ref.shape[0]
    for target in range(team_count):
        column = pl.ds(target % TEAM * HD, HD)
        payload_ref[target, pl.ds(0, prefix), pl.ds(0, HD)] = ck_ref[:, column]
        payload_ref[target, pl.ds(0, prefix), pl.ds(HD, HD)] = cv_ref[:, column]
        payload_ref[target, pl.ds(prefix, NOTE_ROWS), :] = lists_ref[...]


def pack(team_count, lists, caches):
    prefix = caches[0].shape[0]
    note = jnp.pad(lists.astype(jnp.bfloat16)[None, :], ((0, NOTE_ROWS - 1), (0, 2 * HD - lists.shape[0])))
    return pl.pallas_call(
        functools.partial(pack_kernel, team_count),
        out_shape=jax.ShapeDtypeStruct(
            (team_count, prefix + NOTE_ROWS, 2 * HD), jnp.bfloat16
        ),
        in_specs=[VMEM] * 3,
        out_specs=VMEM,
        compiler_params=pltpu.CompilerParams(vmem_limit_bytes=14 * MIB),
        name="pack",
    )(note, *caches)


def turned(value, cosine, sine):
    return value * cosine + pltpu.roll(value, HD // 2, 1) * sine


def heads_kernel(far, first_row, x_count, piece_count, *refs):
    refs = list(refs)

    def take(count):
        taken = refs[:count]
        del refs[:count]
        return taken

    place_ref, lists_ref = take(2)
    x_refs = take(x_count)
    gain_ref, bias_ref, table_ref, cache_ref = take(4)
    cache_value_t_ref, w_ref = take(2)
    piece_refs = take(piece_count)
    (out_ref,) = take(1)
    if piece_count:
        (w_ref,) = take(1)
    q_buf, key_buf, value_t_buf, sem = take(4)

    rows = sum(x_ref.shape[0] for x_ref in x_refs)
    group = place_ref[0]
    copies = []
    if piece_count:
        for index, piece in enumerate(piece_refs):
            start = pl.multiple_of(place_ref[place_ref.shape[0] - 3 + index], 16)
            copies.append((piece, w_ref.at[pl.ds(start, piece.shape[0]), :]))
        copies = start_all(copies, sem)
    blocks_each = (cache_ref.shape[1] - NOTE_ROWS) // QBLK

    def cached(place):
        if blocks_each == 1:
            return place, pl.ds(0, QBLK)
        return place // blocks_each, pl.ds(pl.multiple_of(place % blocks_each * QBLK, QBLK), QBLK)

    factor = HD ** (-0.5) * float(np.log2(np.e))
    causal = lax.broadcasted_iota(jnp.int32, (QBLK, QBLK), 0) <= lax.broadcasted_iota(
        jnp.int32, (QBLK, QBLK), 1
    )
    contract_last = (((1,), (1,)), ((), ()))
    blocks = rows // QBLK

    (x_ref,) = x_refs
    others = (place_ref.shape[0] - 3) // 2
    shard = x_ref.shape[1] // (others + 1)
    if piece_count and shard % HD == 0:
        pairs = [(place_ref[2 + 2 * i], place_ref[3 + 2 * i]) for i in range(others)]
        starts = [place_ref[1]] + [jnp.minimum(*pair) for pair in pairs]
        lin = bias_ref[...]
        for index, start in enumerate(starts):
            if index == others:
                for copy in copies:
                    copy.wait()
            run = pl.ds(pl.multiple_of(start, HD), shard)
            lin = lin + jnp.dot(x_ref[:, run], w_ref[run, :], preferred_element_type=jnp.float32)
    else:
        for copy in copies:
            copy.wait()
        lin = jnp.dot(x_ref[...], w_ref[...], preferred_element_type=jnp.float32)
        lin = lin + bias_ref[...]
    low_half = lax.broadcasted_iota(jnp.int32, (rows, HD), 1) < HD // 2
    all_rows = table_ref.shape[0] // len(FARS)
    table = table_ref[pl.ds(FARS.index(far) * all_rows + first_row, rows), :]
    swapped = pltpu.roll(table, HD // 2, 1)
    cosine = jnp.where(low_half, table, swapped)
    sine = jnp.where(low_half, -swapped, table)
    for tile in range(TILES):
        value = lin[:, tile * HD : (tile + 1) * HD]
        if tile != 1:
            value = turned(value, cosine, sine)
        if tile >= 2:
            q_buf[:, pl.ds((tile - 2) * HD, HD)] = value.astype(jnp.bfloat16)
            continue
        out_ref[:, pl.ds(tile * HD, HD)] = value.astype(out_ref.dtype)
        if tile == 0:
            key_buf[...] = value.astype(jnp.bfloat16)
        else:
            value_t_buf[...] = value.astype(jnp.bfloat16).T

    owner_list = (place_ref[place_ref.shape[0] - 1] ^ far) // 2
    for block in range(blocks):
        span = pl.ds(block * QBLK, QBLK)
        for head in range(GROUP):
            query = q_buf[span, pl.ds(head * HD, HD)]
            listed = (group * GROUP + head) * (all_rows // QBLK) + first_row // QBLK + block
            at = listed * SEL
            slots = [lists_ref[owner_list, at + j] for j in range(SEL)]
            keys = [key_buf[span, :]]
            values = [value_t_buf[:, span]]
            for slot in slots:
                place = jnp.maximum(slot, 0)
                owner, part = cached(place)
                keys.append(cache_ref[owner, part, pl.ds(0, HD)])
                values.append(cache_value_t_ref[place])
            scores = lax.dot_general(
                jnp.concatenate(keys, axis=0),
                query,
                contract_last,
                preferred_element_type=jnp.float32,
            )
            parts = [jnp.where(causal, scores[:QBLK], -jnp.inf)]
            for j in range(SEL):
                part = scores[(j + 1) * QBLK : (j + 2) * QBLK]
                parts.append(part + jnp.where(slots[j] >= 0, 0.0, -jnp.inf))
            top = functools.reduce(jnp.maximum, parts)
            top = jnp.max(top, axis=0, keepdims=True) * factor
            parts = [jnp.exp2(part * factor - top) for part in parts]
            total = jnp.sum(functools.reduce(jnp.add, parts), axis=0, keepdims=True)
            weights = jnp.concatenate([part.astype(jnp.bfloat16) for part in parts], axis=0)
            mixed = jnp.dot(
                jnp.concatenate(values, axis=1), weights, preferred_element_type=jnp.float32
            )
            out_ref[span, pl.ds((2 + head) * HD, HD)] = (mixed / total).T.astype(out_ref.dtype)


def heads(far, first_row, place, lists, x_parts, gain, bias, table, cache, pieces, kept):
    depth = x_parts[0].shape[1]
    rows = sum(part.shape[0] for part in x_parts)
    operands = [place, lists, *x_parts, gain, bias, table, cache]
    specs = [SMEM] * 2 + [VMEM] * (len(x_parts) + 4)
    shapes = [jax.ShapeDtypeStruct((rows, WIDTH), jnp.bfloat16 if far else jnp.float32)]
    operands += kept
    specs += [VMEM] * 2
    aliases = {}
    if pieces:
        aliases = {len(operands) - 1: 1}
        operands += pieces
        specs += [ANY] * len(pieces)
        shapes.append(jax.ShapeDtypeStruct((depth, WIDTH), jnp.bfloat16))
    return pl.pallas_call(
        functools.partial(heads_kernel, far, first_row, len(x_parts), len(pieces)),
        out_shape=shapes,
        in_specs=specs,
        out_specs=[VMEM] * len(shapes),
        input_output_aliases=aliases,
        scratch_shapes=[
            pltpu.VMEM((rows, GROUP * HD), jnp.bfloat16),
            pltpu.VMEM((rows, HD), jnp.bfloat16),
            pltpu.VMEM((HD, rows), jnp.bfloat16),
            pltpu.SemaphoreType.DMA((max(len(pieces), 1),)),
        ],
        compiler_params=pltpu.CompilerParams(vmem_limit_bytes=16 * MIB),
        cost_estimate=pl.CostEstimate(flops=1, bytes_accessed=1, transcendentals=0),
        name="heads",
    )(*operands)


def finish_kernel(runs, place_ref, *refs):
    context_ref, keys_ref, values_ref = refs[-3:]
    for (far, first_row), part in zip(runs, refs):
        rows = pl.ds(first_row, part.shape[0])
        sources = tile_sources(place_ref[0] ^ (far // 2))
        for target, (column, tiles, at) in zip((keys_ref, values_ref, context_ref), sources):
            target[rows, pl.ds(pl.multiple_of(column, HD), tiles * HD)] = part[
                :, pl.ds(at * HD, tiles * HD)
            ].astype(jnp.float32)


def finish(place, rows, parts):
    return pl.pallas_call(
        functools.partial(finish_kernel, tuple(parts)),
        out_shape=[
            jax.ShapeDtypeStruct((rows, TEAM * width), jnp.float32)
            for width in (GROUP * HD, HD, HD)
        ],
        in_specs=[SMEM] + [VMEM] * len(parts),
        out_specs=[VMEM] * 3,
        compiler_params=pltpu.CompilerParams(vmem_limit_bytes=16 * MIB),
        name="finish",
    )(place, *parts.values())


def last_kernel(runs, place_ref, *refs):
    count = len(runs)
    outs, wides, sem = refs[count + 3 : count + 6], refs[count + 6 : -1], refs[-1]
    copies = []
    for (far, first_row), part_ref, wide in zip(runs, refs, wides):
        rows = pl.ds(first_row, part_ref.shape[0])
        for index, (column, tiles, at) in enumerate(tile_sources(place_ref[0] ^ (far // 2))):
            span = pl.ds(at * HD, tiles * HD)
            wide[:, span] = part_ref[:, span].astype(jnp.float32)
            column = pl.ds(pl.multiple_of(column, HD), tiles * HD)
            copy = pltpu.make_async_copy(
                wide.at[:, span], outs[(1, 2, 0)[index]].at[rows, column], sem.at[len(copies)]
            )
            copy.start()
            copies.append(copy)
    for copy in copies:
        copy.wait()


def finish_last(place, parts, outs):
    count = len(parts)
    return pl.pallas_call(
        functools.partial(last_kernel, tuple(parts)),
        out_shape=[jax.ShapeDtypeStruct(out.shape, out.dtype) for out in outs],
        in_specs=[SMEM] + [VMEM] * count + [ANY] * 3,
        out_specs=[ANY] * 3,
        input_output_aliases={1 + count + index: index for index in range(3)},
        scratch_shapes=[pltpu.VMEM(part.shape, jnp.float32) for part in parts.values()]
        + [pltpu.SemaphoreType.DMA((3 * count,))],
        compiler_params=pltpu.CompilerParams(vmem_limit_bytes=16 * MIB),
        name="finish_last",
    )(place, *parts.values(), *outs)


tie = lax.optimization_barrier


def on_device(
    tokens,
    norm_gain,
    w_query,
    w_key,
    w_value,
    b_query,
    b_key,
    b_value,
    cache_keys,
    cache_values,
    block_lists,
    start_position,
):
    rows = tokens.shape[0]
    shard = w_query.shape[0]
    ctx_size, grp_size = lax.axis_size("ctx"), lax.axis_size("grp")
    me, layer = lax.axis_index("ctx"), lax.axis_index("grp")
    group = me // 2 % TEAM
    core = me % 2
    piece_rows = shard // 2

    tokens_2 = swap(tokens, "ctx", 2)
    tokens_4 = swap(tokens, "ctx", 4)
    low, high = tokens_2[: rows // 2], tokens_4[rows // 2 :]

    grp_order = [0]
    for bit in bits_of(grp_size, 1):
        grp_order += [far ^ bit for far in grp_order]
    piece_places = [(far, over) for far in sorted(grp_order) if far for over in (0, 1)]
    place = jnp.stack(
        [group, layer * shard]
        + [(layer ^ far) * shard + (core ^ over) * piece_rows for far, over in piece_places]
        + [me]
    ).astype(jnp.int32)
    weights = (w_key, w_value, w_query)
    half, whole = cut(weights)

    payload = pack(ctx_size // 2, block_lists.reshape(-1), (cache_keys, cache_values))
    same_core = [list(range(c, ctx_size, 2)) for c in range(2)]
    cache = lax.all_to_all(payload, "ctx", 0, 0, axis_index_groups=same_core)
    row_ids = jnp.arange(rows, dtype=jnp.int32)
    tables = rope_table(
        start_position[0]
        + jnp.concatenate([((me ^ far) * grp_size + layer) * rows + row_ids for far in FARS])
    )
    bias = jnp.concatenate(
        [
            lax.dynamic_slice_in_dim(b_key, group * HD, HD),
            lax.dynamic_slice_in_dim(b_value, group * HD, HD),
            lax.dynamic_slice_in_dim(b_query, group * GROUP * HD, GROUP * HD),
        ]
    ).astype(jnp.float32)[None, :]

    tokens_6 = [swap(low, "ctx", 4), swap(high, "ctx", 2)]
    held = {0: half}
    for index, bit in enumerate(bits_of(grp_size, 1)):
        for far in sorted(held):
            held[far ^ bit] = swap(held[far], "grp", bit)
        if index == 0:
            held[bit], tables, bias, cache, *_ = tie((held[bit], tables, bias, cache, low, high))
    lists = cache[:, cache_keys.shape[0], :].astype(jnp.int32)
    blocks_each = cache_keys.shape[0] // QBLK
    owner = jnp.maximum(lists, 0) // blocks_each
    owner = ((owner ^ me) & 1) * (ctx_size // 2) + owner // 2
    lists = jnp.where(lists < 0, -1, owner * blocks_each + jnp.maximum(lists, 0) % blocks_each)
    cache = jnp.concatenate([cache, swap(cache, "ctx", 1)], axis=0)
    last_far = max(held)
    normed = norm(norm_gain[None, :], [tokens_2, tokens_4, tokens])
    held[last_far], *_ = tie((held[last_far], *tokens_6, cache, *normed))
    pieces = [whole]
    for far, over in piece_places:
        pieces.append(swap(held[far], "ctx", 1) if over else held[far])


    early, late = pieces[:-2], pieces[-2:]
    w_part, cache_value_t, normed_6 = gather(
        place, norm_gain[None, :], cache, early, tokens_6
    )
    late[0], tokens_6 = tie((late[0], tokens_6))
    runs = {
        (6, 0): normed_6,
        (2, 0): normed[0],
        (4, 0): normed[1],
        (0, 0): normed[2],
    }
    kept, parts = [cache_value_t, w_part], {}
    for (far, first_row), x in runs.items():
        out, *rest = heads(
            far,
            first_row,
            place,
            lists,
            [x],
            norm_gain[None, :],
            bias,
            tables,
            cache,
            late,
            kept,
        )
        if rest:
            late, kept = [], [cache_value_t, rest[0]]
        parts[(far, first_row)] = swap(out, "ctx", far) if far else out
    first = {run: parts[run] for run in parts if run[0] in (0, 6)}
    last = {run: parts[run] for run in parts if run[0] in (2, 4)}
    return tuple(finish_last(place, last, finish(place, rows, first)))


def solution(mesh):
    in_specs = (
        P(("ctx", "grp"), None),
        P(),
        P("grp", None),
        P("grp", None),
        P("grp", None),
        P(),
        P(),
        P(),
        P("ctx", None),
        P("ctx", None),
        P(None, ("ctx", "grp"), None),
        P(),
    )
    out_specs = (P(("ctx", "grp"), None), P(("ctx", "grp"), None), P(("ctx", "grp"), None))
    return jax.shard_map(
        on_device, mesh=mesh, in_specs=in_specs, out_specs=out_specs, check_vma=False
    )
```
